32 devices in a mesh: seq: 16 (over z, x, core), head: 2 (over y).
Axes of the slice: x: 2, y: 2, z: 4, core: 2. Of those that a mesh axis runs over, the one named last changes fastest.
Arguments:
- tokens: bfloat16 [2, 1024, 1536], P(None, 'seq'), may hold values from -6 to 6
- w_query: bfloat16 [1536, 1536], P('seq', 'head'), may hold values from -0.15625 to 0.15625
- w_key: bfloat16 [1536, 1536], P('seq', 'head'), may hold values from -0.15625 to 0.15625
- w_value: bfloat16 [1536, 1536], P('seq', 'head'), may hold values from -0.15625 to 0.15625
- w_house: bfloat16 [1536, 1536], P('seq', 'head'), may hold values from -0.15625 to 0.15625
- w_beta: bfloat16 [1536, 12], P('seq', 'head'), may hold values from -0.15625 to 0.15625
- beta_bias: float32 [12], P('head'), may hold values from -4 to 4
- w_out: bfloat16 [1536, 1536], P('head', 'seq'), may hold values from -0.625 to 0.625
- w_gate: bfloat16 [1536, 4096], P('seq', 'head'), may hold values from -0.15625 to 0.15625
- w_up: bfloat16 [1536, 4096], P('seq', 'head'), may hold values from -0.15625 to 0.15625
- w_down: bfloat16 [4096, 1536], P('head', 'seq'), may hold values from -0.09375 to 0.09375
- gain_attn: float32 [1536], replicated, may hold values from 0.5 to 1.5
- gain_mlp: float32 [1536], replicated, may hold values from 0.5 to 1.5
- segment_ids: int32 [2, 1024], P(None, 'seq'), may hold values from 0 to 3, as said below
- out_grad: bfloat16 [2, 1024, 1536], P(None, 'seq'), may hold values from -6 to 6
Outputs:
- block_out: bfloat16 [2, 1024, 1536], P(None, 'seq')
- tokens_grad: float32 [2, 1024, 1536], P(None, 'seq')
- query_grad: float32 [1536, 1536], P('seq', 'head')
- key_grad: float32 [1536, 1536], P('seq', 'head')
- value_grad: float32 [1536, 1536], P('seq', 'head')
- house_grad: float32 [1536, 1536], P('seq', 'head')
- beta_grad: float32 [1536, 12], P('seq', 'head')
- bias_grad: float32 [12], P('head')
- out_weight_grad: float32 [1536, 1536], P('head', 'seq')
- gate_grad: float32 [1536, 4096], P('seq', 'head')
- up_grad: float32 [1536, 4096], P('seq', 'head')
- down_grad: float32 [4096, 1536], P('head', 'seq')
- attn_gain_grad: float32 [1536], replicated
- mlp_gain_grad: float32 [1536], replicated
The draws below stay inside these ranges and needn't reach their ends.
Inputs may be any that keep to these rules, and one draw needn't show every extreme that they name: `segment_ids`: along each micro-batch the ids start at 0 and rise by one at each new sequence; the first rise lies within the first 64 positions and the last within the last 64; one micro-batch, drawn from the seed, holds three sequences, the others four.
All inputs are finite; a program needn't handle non-finite values.
Results may differ from the reference program's by a relative error of at most 0.012.
The reference program's roundings to bfloat16 on the way count: a program that leaves them out, or rounds other values in their place, can miss the bound.
Values may be sent and summed in bfloat16 or wider, within the bound.
No kernel may reach another device: no remote copies, remote signals or barrier semaphores. Data moves between devices by JAX's collectives and lax.ppermute only.
A program may use at most 192 MiB of HBM per device.

```python
import jax
import jax.numpy as jnp
from jax import lax

D = 1536
HEADS = 12
HD = 128
FF = 4096
TOK_DEV = 64
MICRO = 2
TOKENS = 1024


def draw_segment_ids(key, part):
    key = jax.random.fold_in(key, 7)
    first_key, last_key, middle_key, pick_key = jax.random.split(key, 4)
    first_cut = jax.random.randint(first_key, (MICRO, 1), 1, TOK_DEV)
    last_cut = jax.random.randint(last_key, (MICRO, 1), TOKENS - TOK_DEV + 1, TOKENS)
    middle_cut = jax.random.randint(middle_key, (MICRO, 1), first_cut + 1, last_cut)
    spanning = jax.random.randint(pick_key, (), 0, MICRO)
    position = jnp.arange(TOKENS, dtype=jnp.int32)[None, :]
    split_more = (jnp.arange(MICRO, dtype=jnp.int32)[:, None] != spanning).astype(jnp.int32)
    return (position >= first_cut).astype(jnp.int32) + (position >= last_cut).astype(jnp.int32) + split_more * (position >= middle_cut).astype(jnp.int32)


def steps_of(own_key, extent, shards, low, largest):
    level, own = 1.0, jax.random.fold_in(own_key, 6)
    for dim, parts in shards:
        steps = jnp.exp(jax.random.uniform(jax.random.fold_in(own, dim), (parts,), jnp.float32, low / len(shards), largest / len(shards)))
        level = level * jnp.repeat(steps, extent[dim] // parts).reshape([-1 if axis == dim else 1 for axis in range(len(extent))])
    return level


def normal_values(rng, extent, deviation, bound, shards=(), held_as=jnp.bfloat16):
    gain = steps_of(rng, extent, shards, -0.22, 0.18) if shards else 1.0
    result = jax.random.normal(rng, extent, jnp.float32) * deviation * gain
    return jnp.minimum(jnp.maximum(result, -bound), bound).astype(held_as)


def setup_inputs(seed: int = 0) -> dict:
    key_of = jax.random.split(jax.random.key(seed), 16)
    return {
        "tokens": normal_values(key_of[0], (MICRO, TOKENS, D), 1.0, 6.0, ((1, 16),)),
        "w_query": normal_values(key_of[1], (D, D), D ** -0.5, 0.15625, ((0, 16), (1, 2))),
        "w_key": normal_values(key_of[2], (D, D), D ** -0.5, 0.15625, ((0, 16), (1, 2))),
        "w_value": normal_values(key_of[3], (D, D), D ** -0.5, 0.15625, ((0, 16), (1, 2))),
        "w_house": normal_values(key_of[4], (D, D), D ** -0.5, 0.15625, ((0, 16), (1, 2))),
        "w_beta": normal_values(key_of[5], (D, HEADS), D ** -0.5, 0.15625, ((0, 16), (1, 2))),
        "beta_bias": jnp.clip(jax.random.uniform(key_of[6], (HEADS,), jnp.float32, -4.0, 4.0) * steps_of(key_of[6], (HEADS,), ((0, 2),), -0.4, 0.0), -4.0, 4.0),
        "w_out": normal_values(key_of[7], (D, D), (D // 16) ** -0.5, 0.625, ((0, 2), (1, 16))),
        "w_gate": normal_values(key_of[8], (D, FF), D ** -0.5, 0.15625, ((0, 16), (1, 2))),
        "w_up": normal_values(key_of[9], (D, FF), D ** -0.5, 0.15625, ((0, 16), (1, 2))),
        "w_down": normal_values(key_of[10], (FF, D), FF ** -0.5, 0.09375, ((0, 2), (1, 16))),
        "gain_attn": jnp.clip(1.0 + 0.1 * jax.random.normal(key_of[11], (D,), jnp.float32), 0.5, 1.5),
        "gain_mlp": jnp.clip(1.0 + 0.1 * jax.random.normal(key_of[12], (D,), jnp.float32), 0.5, 1.5),
        "segment_ids": draw_segment_ids(jax.random.fold_in(key_of[15], 71), 0),
        "out_grad": normal_values(key_of[14], (MICRO, TOKENS, D), 1.0, 6.0, ((1, 16),)),
    }


highest = lax.Precision.HIGHEST
epsilon = 1e-06
masked_score = -1e+30

@jax.custom_vjp
def low(v):
    return lax.optimization_barrier(v.astype(jnp.bfloat16)).astype(jnp.float32)

@jax.custom_vjp
def low_back(v):
    return v

def low_keep(v):
    return (low(v), None)

def low_pass(kept, grad):
    return (grad,)

def back_keep(v):
    return (v, None)

def back_low(kept, grad):
    return (low(grad),)
low.defvjp(low_keep, low_pass)
low_back.defvjp(back_keep, back_low)

def normalize(values):
    return values * lax.rsqrt(lax.optimization_barrier(jnp.mean(values * values, axis=-1, keepdims=True)) + epsilon)

def block_factors(house_raw, beta_logit):
    mirror = house_raw * lax.rsqrt(lax.optimization_barrier(jnp.sum(house_raw * house_raw, axis=-1, keepdims=True)) + epsilon)
    strength = 2.0 * jax.nn.sigmoid(beta_logit)
    length = mirror.shape[-2]
    inner_dots = jnp.einsum('...td,...sd->...ts', mirror, mirror, precision=highest)
    strict_lower = jnp.tril(jnp.ones((length, length), jnp.float32), -1)
    system = jnp.eye(length, dtype=jnp.float32) + strength[..., :, None] * inner_dots * strict_lower
    diagonal = jnp.eye(length, dtype=jnp.float32) * strength[..., None, :]
    triang = jax.scipy.linalg.solve_triangular(system, diagonal, lower=True, unit_diagonal=True)
    return (mirror, triang)

def local_terms(queries, key_vecs, mirror, triang):
    length = queries.shape[-2]
    lower_incl = jnp.tril(jnp.ones((length, length), jnp.float32))
    query_dots = jnp.einsum('...id,...td->...it', queries, mirror, precision=highest) * lower_incl
    key_dots = jnp.einsum('...jd,...td->...jt', key_vecs, mirror, precision=highest) * (1.0 - lower_incl)
    query_mix = jnp.einsum('...it,...ts->...is', query_dots, triang, precision=highest)
    moved_query = queries - jnp.einsum('...is,...sd->...id', query_mix, mirror, precision=highest)
    key_mix = jnp.einsum('...js,...ts->...jt', key_dots, triang, precision=highest)
    moved_key = key_vecs - jnp.einsum('...jt,...td->...jd', key_mix, mirror, precision=highest)
    logits = jnp.einsum('...id,...jd->...ij', queries, key_vecs, precision=highest)
    logits = logits - jnp.einsum('...is,...js->...ij', query_mix, key_dots, precision=highest)
    return (moved_query, moved_key, logits)

def transform(keys_in, mirror, triang):
    key_dots = jnp.einsum('...jd,...sd->...js', keys_in, mirror, precision=highest)
    key_mix = jnp.einsum('...js,...ts->...jt', key_dots, triang, precision=highest)
    return keys_in - jnp.einsum('...jt,...td->...jd', key_mix, mirror, precision=highest)

def attend_head(packed):
    queries, key_vecs, value_vecs, house_raw, beta_logit, labels = packed
    blocks = labels.shape[0] // TOK_DEV

    def to_blocks(values):
        return values.reshape(blocks, TOK_DEV, HD)
    query_b = to_blocks(queries)
    key_b = to_blocks(key_vecs)
    value_b = to_blocks(value_vecs)
    label_b = labels.reshape(blocks, TOK_DEV)
    mirror, triang = block_factors(to_blocks(house_raw), beta_logit.reshape(blocks, TOK_DEV))
    moved_query, moved_key, logits = local_terms(query_b, key_b, mirror, triang)
    score_scale = HD ** (-0.5)
    causal = jnp.tril(jnp.ones((TOK_DEV, TOK_DEV), jnp.bool_))
    allowed = causal[None] & (label_b[:, :, None] == label_b[:, None, :])
    scores = jnp.where(allowed, logits * score_scale, masked_score)
    running_max = lax.optimization_barrier(jnp.max(scores, axis=-1))
    weights = jnp.exp(scores - running_max[..., None])
    running_sum = lax.optimization_barrier(jnp.sum(weights, axis=-1))
    running_out = jnp.einsum('bij,bjd->bid', weights, value_b, precision=highest)
    value_pad = jnp.concatenate([jnp.zeros_like(value_b), value_b], axis=0)
    label_pad = jnp.concatenate([jnp.zeros_like(label_b), label_b], axis=0)

    def cross_turn(carried, distance):
        old_max, old_sum, old_out, keys_out = carried
        keys_in = jnp.concatenate([jnp.zeros_like(keys_out[:1]), keys_out[:-1]], axis=0)
        start_at = (blocks - distance).astype(jnp.int32)
        values_in = lax.dynamic_slice_in_dim(value_pad, start_at, blocks, 0)
        labels_in = lax.dynamic_slice_in_dim(label_pad, start_at, blocks, 0)
        cross = jnp.einsum('bid,bjd->bij', moved_query, keys_in, precision=highest) * score_scale
        cross = jnp.where(label_b[:, :, None] == labels_in[:, None, :], cross, masked_score)
        new_max = jnp.maximum(old_max, lax.optimization_barrier(jnp.max(cross, axis=-1)))
        factor = jnp.exp(old_max - new_max)
        cross_weights = jnp.exp(cross - new_max[..., None])
        new_sum = old_sum * factor + lax.optimization_barrier(jnp.sum(cross_weights, axis=-1))
        new_out = old_out * factor[..., None] + jnp.einsum('bij,bjd->bid', cross_weights, values_in, precision=highest)
        return ((new_max, new_sum, new_out, transform(keys_in, mirror, triang)), None)
    final_state = lax.scan(jax.checkpoint(cross_turn), (running_max, running_sum, running_out, moved_key), jnp.arange(1, blocks, dtype=jnp.int32))[0]
    return (final_state[2] / final_state[1][..., None]).reshape(blocks * TOK_DEV, HD)

def attention_all(queries, key_vecs, value_vecs, house_raw, beta_logit, segment_ids):
    batches, length = segment_ids.shape

    def heads_first(values):
        return values.reshape(batches, length, HEADS, HD).transpose(0, 2, 1, 3).reshape(batches * HEADS, length, HD)
    logit_rows = beta_logit.transpose(0, 2, 1).reshape(batches * HEADS, length)
    labels = jnp.broadcast_to((segment_ids + 1)[:, None, :], (batches, HEADS, length)).reshape(batches * HEADS, length)
    results = lax.map(jax.checkpoint(attend_head), (heads_first(queries), heads_first(key_vecs), heads_first(value_vecs), heads_first(house_raw), logit_rows, labels))
    return results.reshape(batches, HEADS, length, HD).transpose(0, 2, 1, 3).reshape(batches, length, HEADS * HD)

def forward(inputs, w_query, w_key, w_value, w_house, w_beta, beta_bias, w_out, w_gate, w_up, w_down, gain_attn, gain_mlp, segment_ids):

    def project(values, weight):
        return jnp.einsum('mtd,de->mte', values, weight, precision=highest)
    attn_in = low(normalize(inputs) * gain_attn)
    queries = low_back(project(attn_in, w_query))
    key_vecs = low_back(project(attn_in, w_key))
    value_vecs = low_back(project(attn_in, w_value))
    house_raw = low_back(project(attn_in, w_house))
    beta_logit = low_back(project(attn_in, w_beta) + beta_bias)
    attended = low(attention_all(queries, key_vecs, value_vecs, house_raw, beta_logit, segment_ids))
    middle = inputs + low_back(project(attended, w_out))
    mlp_in = low(normalize(middle) * gain_mlp)
    gate_proj = low_back(project(mlp_in, w_gate))
    up_proj = low_back(project(mlp_in, w_up))
    hidden = low(jax.nn.silu(gate_proj) * up_proj)
    return middle + low_back(project(hidden, w_down))

def reference(tokens, w_query, w_key, w_value, w_house, w_beta, beta_bias, w_out, w_gate, w_up, w_down, gain_attn, gain_mlp, segment_ids, out_grad):
    floats = [array.astype(jnp.float32) for array in (tokens, w_query, w_key, w_value, w_house, w_beta, beta_bias, w_out, w_gate, w_up, w_down, gain_attn, gain_mlp)]

    def closed_forward(*params):
        return forward(*params, segment_ids)
    block_out, pullback = jax.vjp(closed_forward, *floats)
    gradients = pullback(out_grad.astype(jnp.float32))
    return (block_out.astype(jnp.bfloat16), gradients[0], gradients[1], gradients[2], gradients[3], gradients[4], gradients[5], gradients[6], gradients[7], gradients[8], gradients[9], gradients[10], gradients[11], gradients[12])
```

```python
import functools

import jax
import jax.numpy as jnp
from jax import lax
from jax.experimental import pallas as pl
from jax.experimental.pallas import tpu as pltpu
from jax.sharding import Mesh
from jax.sharding import PartitionSpec as P

epsilon = 1e-06
masked_score = -1e30
MERGE_LIMIT = 2048
LEAF = 128
NN, NT, TN = ((1,), (0,)), ((1,), (1,)), ((0,), (0,))


def split(a):
    if isinstance(a, tuple):
        return a
    if a.dtype == jnp.bfloat16:
        return (a, None)
    high = a.astype(jnp.bfloat16)
    return (high, (a - high.astype(jnp.float32)).astype(jnp.bfloat16))


def raw_dot(a, b, dims):
    return lax.dot_general(a, b, (dims, ((), ())), preferred_element_type=jnp.float32)


def dot_parts(a, b, dims):
    (ah, al), (bh, bl) = split(a), split(b)
    total = raw_dot(ah, bh, dims)
    if bl is not None:
        total = total + raw_dot(ah, bl, dims)
    if al is not None:
        total = total + raw_dot(al, bh, dims)
    return total


def grid_of(shape, axis):
    return lax.broadcasted_iota(jnp.int32, shape, axis)


def leaf_masks():
    row, col = grid_of((LEAF, LEAF), 0), grid_of((LEAF, LEAF), 1)
    return row, col


def leaf_forward_kernel(leaves, q_ref, k_ref, h_ref, g_ref, x_out, a_out, c_out, u_out, w_out, tm_out, dots_out, own_out, qm_out, km_out, p_out):
    mm = dot_parts
    row, col = leaf_masks()
    eye = (row == col).astype(jnp.float32)
    span = range(leaves)
    at = [pl.ds(g * LEAF, LEAF) for g in span]
    q = [split(q_ref[i, :]) for i in at]
    k = [split(k_ref[i, :]) for i in at]
    mirror, strength = [], []
    for i in at:
        h = h_ref[i, :]
        mirror.append(split(h * lax.rsqrt(jnp.sum(h * h, axis=-1, keepdims=True) + epsilon)))
        strength.append(2.0 * jax.nn.sigmoid(jnp.broadcast_to(g_ref[i, 0:1], (LEAF, LEAF))))
    dots = [mm(m, m, NT) for m in mirror]
    system = [jnp.where(row > col, d, 0.0) * s for d, s in zip(dots, strength)]
    inverse = [eye - jnp.where((row // 2 == col // 2), n, 0.0) for n in system]
    width = 2
    while width < LEAF:
        picked = (row // (2 * width) == col // (2 * width)) & (row // width != col // width)
        parts = [split(x) for x in inverse]
        off = [split(jnp.where(picked, n, 0.0)) for n in system]
        turned = [mm(x, n, NN) for x, n in zip(parts, off)]
        inverse = [x - mm(t, p, NN) for x, t, p in zip(inverse, turned, parts)]
        width *= 2
    triang = [split(x * s.T) for x, s in zip(inverse, strength)]
    a_part = [split(jnp.where(row >= col, mm(x, m, NT), 0.0)) for x, m in zip(q, mirror)]
    c_part = [split(jnp.where(row < col, mm(x, m, NT), 0.0)) for x, m in zip(k, mirror)]
    own = [mm(x, y, NT) for x, y in zip(q, k)]
    u_part = [split(mm(x, t, NN)) for x, t in zip(a_part, triang)]
    w_part = [split(mm(x, t, NT)) for x, t in zip(c_part, triang)]
    tm_part = [split(mm(t, m, NN)) for t, m in zip(triang, mirror)]
    for g, i in enumerate(at):
        x_out[i, :] = inverse[g]
        dots_out[i, :] = dots[g]
        for ref, value in ((a_out, a_part), (c_out, c_part), (u_out, u_part), (w_out, w_part), (tm_out, tm_part)):
            high, low = value[g]
            ref[i, :] = high.astype(jnp.float32) + low.astype(jnp.float32)
        own_out[i, :] = own[g] - mm(u_part[g], c_part[g], NT)
        qm_out[i, :] = q_ref[i, :] - mm(u_part[g], mirror[g], NN)
        km_out[i, :] = k_ref[i, :] - mm(w_part[g], mirror[g], NN)
        p_out[i, :] = eye - mm(mirror[g], tm_part[g], TN)


def leaf_backward_kernel(leaves, q_ref, k_ref, h_ref, g_ref, x_ref, a_ref, c_ref, u_ref, w_ref, tm_ref, dots_ref, gown_ref, gqm_ref, gkm_ref, gp_ref, dv_ref, out):
    mm = dot_parts
    row, col = leaf_masks()
    ones = jnp.ones((LEAF, LEAF), jnp.bfloat16)
    at = [pl.ds(g * LEAF, LEAF) for g in range(leaves)]
    q = [split(q_ref[i, :]) for i in at]
    k = [split(k_ref[i, :]) for i in at]
    h = [h_ref[i, :] for i in at]
    scaling = [lax.rsqrt(jnp.sum(x * x, axis=-1, keepdims=True) + epsilon) for x in h]
    mirror_full = [x * r for x, r in zip(h, scaling)]
    mirror = [split(x) for x in mirror_full]
    strength = [2.0 * jax.nn.sigmoid(jnp.broadcast_to(g_ref[i, 0:1], (LEAF, LEAF))) for i in at]
    inverse_full = [x_ref[i, :] for i in at]
    inverse = [split(x) for x in inverse_full]
    strength_row = [s.T for s in strength]
    triang = [split(x * s) for x, s in zip(inverse_full, strength_row)]
    a_part = [split(a_ref[i, :]) for i in at]
    c_part = [split(c_ref[i, :]) for i in at]
    u_part = [split(u_ref[i, :]) for i in at]
    w_part = [split(w_ref[i, :]) for i in at]
    tm_part = [split(tm_ref[i, :]) for i in at]
    gown = [split(gown_ref[i, :]) for i in at]
    gqm = [split(gqm_ref[i, :]) for i in at]
    gkm = [split(gkm_ref[i, :]) for i in at]
    gp = [split(gp_ref[i, :]) for i in at]
    span = range(leaves)
    gu = [split(-mm(gqm[g], mirror[g], NT) - mm(gown[g], c_part[g], NN)) for g in span]
    gw = [split(-mm(gkm[g], mirror[g], NT)) for g in span]
    mgp = [split(mm(mirror[g], gp[g], NN)) for g in span]
    ga = [split(jnp.where(row >= col, mm(gu[g], triang[g], NT), 0.0)) for g in span]
    gc = [split(jnp.where(row < col, mm(gw[g], triang[g], NN) - mm(gown[g], u_part[g], TN), 0.0)) for g in span]
    gt = [mm(a_part[g], gu[g], TN) + mm(gw[g], c_part[g], TN) - mm(mgp[g], mirror[g], NT) for g in span]
    gx = [split(gt[g] * strength_row[g]) for g in span]
    xgx = [split(mm(inverse[g], gx[g], TN)) for g in span]
    gn = [jnp.where(row > col, -mm(xgx[g], inverse[g], NT), 0.0) for g in span]
    gdots = [split(strength[g] * gn[g]) for g in span]
    for g, i in enumerate(at):
        gm = (
            -mm(u_part[g], gqm[g], TN)
            - mm(w_part[g], gkm[g], TN)
            + mm(ga[g], q[g], TN)
            + mm(gc[g], k[g], TN)
            + mm(gdots[g], mirror[g], NN)
            + mm(gdots[g], mirror[g], TN)
            - mm(tm_part[g], gp[g], NT)
            - mm(triang[g], mgp[g], TN)
        )
        gq = gqm_ref[i, :] + mm(gown[g], k[g], NN) + mm(ga[g], mirror[g], NN)
        gk = gkm_ref[i, :] + mm(gown[g], q[g], TN) + mm(gc[g], mirror[g], NN)
        gh = scaling[g] * (gm - mirror_full[g] * jnp.sum(gm * mirror_full[g], axis=-1, keepdims=True))
        gs = mm(gn[g] * dots_ref[i, :], ones, NN) + mm(gt[g] * inverse_full[g], ones, TN)
        gl = gs * strength[g] * (1.0 - 0.5 * strength[g])
        out[i, 0:128] = gq.astype(jnp.bfloat16)
        out[i, 128:256] = gk.astype(jnp.bfloat16)
        out[i, 256:384] = dv_ref[i, :].astype(jnp.bfloat16)
        out[i, 384:512] = gh.astype(jnp.bfloat16)
        out[i, 512:640] = jnp.where(col == 0, gl, 0.0).astype(jnp.bfloat16)


def halves(length):
    found, h = [], LEAF
    while h < length:
        found.append(h)
        h *= 2
    return found


def merge_forward(length, scale, own, v, qm, km, p, lab_col, lab_row, attended, lse, levels, m_ref, l_ref, o_ref):
    mm = dot_parts
    row, col = leaf_masks()
    for start in range(0, length, LEAF):
        i = slice(start, start + LEAF)
        allowed = (row >= col) & (lab_col[i, 0:1] == lab_row[:, i])
        scores = jnp.where(allowed, own[i, :] * scale, masked_score)
        top = jnp.max(scores, axis=-1, keepdims=True)
        weights = jnp.exp(scores - top)
        m_ref[i, :] = top
        l_ref[i, :] = jnp.sum(weights, axis=-1, keepdims=True)
        o_ref[i, :] = mm(weights, v[i, :], NN)
    sizes = halves(length)
    for step, h in enumerate(sizes):
        last = step + 1 == len(sizes)
        if not last:
            qm_next, km_next, p_next = levels[step]
        for start in range(0, length, 2 * h):
            a, b = slice(start, start + h), slice(start + h, start + 2 * h)
            pa = slice(start // h * LEAF, start // h * LEAF + LEAF)
            pb = slice(start // h * LEAF + LEAF, start // h * LEAF + 2 * LEAF)
            qm_b, km_a = split(qm[b, :]), split(km[a, :])
            scores = mm(qm_b, km_a, NT) * scale
            scores = jnp.where(lab_col[b, 0:1] == lab_row[:, a], scores, masked_score)
            old = m_ref[b, :]
            top = jnp.maximum(old, jnp.max(scores, axis=-1, keepdims=True))
            factor = jnp.exp(old - top)
            weights = jnp.exp(scores - top)
            m_ref[b, :] = top
            l_ref[b, :] = l_ref[b, :] * factor + jnp.sum(weights, axis=-1, keepdims=True)
            o_ref[b, :] = o_ref[b, :] * factor + mm(weights, v[a, :], NN)
            if not last:
                p_a, p_b = split(p[pa, :]), split(p[pb, :])
                qm_next[a, :] = qm[a, :]
                qm_next[b, :] = mm(qm_b, p_a, NN)
                km_next[b, :] = km[b, :]
                km_next[a, :] = mm(km_a, p_b, NT)
                if p_next is not None:
                    into = start // (2 * h) * LEAF
                    p_next[slice(into, into + LEAF), :] = mm(p_b, p_a, NN)
        if not last:
            qm, km, p = qm_next, km_next, p_next
    total = l_ref[...]
    attended[...] = o_ref[...] / total
    lse[...] = jnp.broadcast_to(m_ref[...] + jnp.log(total), (length, LEAF))


def merge_backward(length, scale, own, v, levels, lab_col, lab_row, attended, lse, dout, gown, gqm, gkm, gp, dv, delta_ref):
    mm = dot_parts
    row, col = leaf_masks()
    delta_ref[...] = jnp.sum(dout[...] * attended[...], axis=-1, keepdims=True)
    for start in range(0, length, LEAF):
        i = slice(start, start + LEAF)
        allowed = (row >= col) & (lab_col[i, 0:1] == lab_row[:, i])
        probs = jnp.where(allowed, jnp.exp(own[i, :] * scale - lse[i, 0:1]), 0.0)
        grad = split(dout[i, :])
        dv[i, :] = mm(probs, grad, TN)
        gown[i, :] = probs * (mm(grad, v[i, :], NT) - delta_ref[i, :]) * scale
    sizes = halves(length)
    for step in reversed(range(len(sizes))):
        h = sizes[step]
        last = step + 1 == len(sizes)
        qm, km, p = levels[step]
        for start in range(0, length, 2 * h):
            a, b = slice(start, start + h), slice(start + h, start + 2 * h)
            pa = slice(start // h * LEAF, start // h * LEAF + LEAF)
            pb = slice(start // h * LEAF + LEAF, start // h * LEAF + 2 * LEAF)
            qm_b, km_a, grad = split(qm[b, :]), split(km[a, :]), split(dout[b, :])
            scores = mm(qm_b, km_a, NT) * scale
            allowed = lab_col[b, 0:1] == lab_row[:, a]
            probs = jnp.where(allowed, jnp.exp(scores - lse[b, 0:1]), 0.0)
            dv[a, :] = dv[a, :] + mm(probs, grad, TN)
            ds = split(probs * (mm(grad, v[a, :], NT) - delta_ref[b, :]) * scale)
            gq_part = mm(ds, km_a, NN)
            gk_part = mm(ds, qm_b, TN)
            if last:
                gqm[a, :] = jnp.zeros((h, LEAF), jnp.float32)
                gkm[b, :] = jnp.zeros((h, LEAF), jnp.float32)
                gqm[b, :] = gq_part
                gkm[a, :] = gk_part
            else:
                p_a, p_b = split(p[pa, :]), split(p[pb, :])
                gq_b, gk_a = split(gqm[b, :]), split(gkm[a, :])
                gp_a, gp_b = mm(qm_b, gq_b, TN), mm(gk_a, km_a, TN)
                if step + 2 < len(sizes):
                    into = start // (2 * h) * LEAF
                    g_up = split(gp[step + 1][slice(into, into + LEAF), :])
                    gp_a, gp_b = gp_a + mm(p_b, g_up, TN), gp_b + mm(g_up, p_a, NT)
                gp[step][pa, :] = gp_a
                gp[step][pb, :] = gp_b
                gqm[b, :] = mm(gq_b, p_a, NT) + gq_part
                gkm[a, :] = mm(gk_a, p_b, NN) + gk_part


def whole_dot(spec, *operands):
    return jnp.einsum(spec, *operands, precision=lax.Precision.HIGHEST)


def pairs(value, size):
    both = value.reshape(-1, 2, size, value.shape[-1])
    return both[:, 0], both[:, 1]


def joined(first, second):
    return jnp.stack([first, second], axis=1).reshape(-1, first.shape[-1])


def long_allowed(label, size, own):
    both = label.reshape(-1, size) if own else label.reshape(-1, 2, size)
    left, right = (both, both) if own else (both[:, 0], both[:, 1])
    same = right[:, :, None] == left[:, None, :]
    return same & jnp.tril(jnp.ones((size, size), jnp.bool_)) if own else same


def long_forward(length, scale, own, v, qm, km, p, label):
    scores = jnp.where(long_allowed(label, LEAF, True), own.reshape(-1, LEAF, LEAF) * scale, masked_score)
    top = jnp.max(scores, axis=-1, keepdims=True)
    weights = jnp.exp(scores - top)
    state = [
        x.reshape(length, -1)
        for x in (top, jnp.sum(weights, axis=-1, keepdims=True), whole_dot("nij,njd->nid", weights, v.reshape(-1, LEAF, LEAF)))
    ]
    levels = []
    for h in halves(length):
        (q_a, q_b), (k_a, k_b), (v_a, _) = pairs(qm, h), pairs(km, h), pairs(v, h)
        scores = whole_dot("nid,njd->nij", q_b, k_a) * scale
        scores = jnp.where(long_allowed(label, h, False), scores, masked_score)
        (m_a, m_b), (l_a, l_b), (o_a, o_b) = (pairs(x, h) for x in state)
        top = jnp.maximum(m_b, jnp.max(scores, axis=-1, keepdims=True))
        factor = jnp.exp(m_b - top)
        weights = jnp.exp(scores - top)
        l_b = l_b * factor + jnp.sum(weights, axis=-1, keepdims=True)
        o_b = o_b * factor + whole_dot("nij,njd->nid", weights, v_a)
        state = [joined(m_a, top), joined(l_a, l_b), joined(o_a, o_b)]
        if 2 * h < length:
            p_a, p_b = pairs(p, LEAF)
            qm = joined(q_a, whole_dot("nid,nde->nie", q_b, p_a))
            km = joined(whole_dot("nid,ned->nie", k_a, p_b), k_b)
            p = whole_dot("nde,nef->ndf", p_b, p_a).reshape(-1, LEAF)
            levels += [qm, km] + ([p] if 4 * h < length else [])
    top, total, out = state
    return [out / total, jnp.broadcast_to(top + jnp.log(total), (length, LEAF))] + levels


def long_backward(length, scale, own, v, levels, label, attended, lse, dout):
    lse = lse[:, :1]
    delta = jnp.sum(dout * attended, axis=-1, keepdims=True)
    blocks = lambda x: x.reshape(length // LEAF, LEAF, -1)
    probs = jnp.exp(blocks(own) * scale - blocks(lse))
    probs = jnp.where(long_allowed(label, LEAF, True), probs, 0.0)
    dv = whole_dot("nij,nid->njd", probs, blocks(dout)).reshape(length, LEAF)
    gown = probs * (whole_dot("nid,njd->nij", blocks(dout), blocks(v)) - blocks(delta)) * scale
    gqm = gkm = gp = None
    for h, (qm, km, p) in reversed(list(zip(halves(length), levels))):
        (_, q_b), (k_a, _), (v_a, _), (_, o_b) = pairs(qm, h), pairs(km, h), pairs(v, h), pairs(dout, h)
        scores = whole_dot("nid,njd->nij", q_b, k_a) * scale - pairs(lse, h)[1]
        probs = jnp.where(long_allowed(label, h, False), jnp.exp(scores), 0.0)
        dv_a, dv_b = pairs(dv, h)
        dv = joined(dv_a + whole_dot("nij,nid->njd", probs, o_b), dv_b)
        ds = probs * (whole_dot("nid,njd->nij", o_b, v_a) - pairs(delta, h)[1]) * scale
        gq_part, gk_part = whole_dot("nij,njd->nid", ds, k_a), whole_dot("nij,nid->njd", ds, q_b)
        if gqm is None:
            gqm, gkm = joined(jnp.zeros_like(gq_part), gq_part), joined(gk_part, jnp.zeros_like(gk_part))
            continue
        (gq_a, gq_b), (gk_a, gk_b), (p_a, p_b) = pairs(gqm, h), pairs(gkm, h), pairs(p, LEAF)
        gp_a, gp_b = whole_dot("nid,nie->nde", q_b, gq_b), whole_dot("nid,nie->nde", gk_a, k_a)
        if gp is not None:
            above = gp.reshape(-1, LEAF, LEAF)
            gp_a = gp_a + whole_dot("nde,ndf->nef", p_b, above)
            gp_b = gp_b + whole_dot("ndf,nef->nde", above, p_a)
        gp = joined(gp_a, gp_b)
        gqm = joined(gq_a, whole_dot("nid,ned->nie", gq_b, p_a) + gq_part)
        gkm = joined(whole_dot("nid,nde->nie", gk_a, p_b) + gk_part, gk_b)
    return [gown.reshape(length, LEAF), gqm, gkm, gp, dv]


def matrix(rows, columns=LEAF, dtype=jnp.float32):
    return jax.ShapeDtypeStruct((rows, columns), dtype)


def cost(flops, moved):
    return pl.CostEstimate(flops=flops, bytes_accessed=moved, transcendentals=0)


def settings():
    return pltpu.CompilerParams(vmem_limit_bytes=56 * 1024 * 1024)


def leaf_group(length):
    leaves = length // LEAF
    return 4 if leaves % 4 == 0 else 1


def leaf_forward(proj):
    length = proj.shape[0]
    leaves = leaf_group(length)
    rows = leaves * LEAF
    column = lambda j: pl.BlockSpec((rows, LEAF), lambda i, j=j: (i, j))
    return pl.pallas_call(
        functools.partial(leaf_forward_kernel, leaves),
        grid=(length // rows,),
        in_specs=[column(0), column(1), column(3), column(4)],
        out_specs=[column(0)] * 11,
        out_shape=[matrix(length)] * 11,
        compiler_params=settings(),
        name="leaf_forward",
    )(proj, proj, proj, proj)


def leaf_backward(proj, saved, grads):
    length = proj.shape[0]
    leaves = leaf_group(length)
    rows = leaves * LEAF
    column = lambda j: pl.BlockSpec((rows, LEAF), lambda i, j=j: (i, j))
    return pl.pallas_call(
        functools.partial(leaf_backward_kernel, leaves),
        grid=(length // rows,),
        in_specs=[column(0), column(1), column(3), column(4)] + [column(0)] * (len(saved) + len(grads)),
        out_specs=pl.BlockSpec((rows, 5 * LEAF), lambda i: (i, 0)),
        out_shape=matrix(length, 5 * LEAF, jnp.bfloat16),
        compiler_params=settings(),
        name="leaf_backward",
    )(proj, proj, proj, proj, *saved, *grads)


def level_shapes(length):
    sizes = halves(length)
    shapes = []
    for step in range(1, len(sizes)):
        shapes += [matrix(length), matrix(length)]
        if step + 1 < len(sizes):
            shapes.append(matrix(length // sizes[step] * LEAF))
    return shapes


def level_groups(length, flat):
    sizes, groups, flat = halves(length), [], list(flat)
    for step in range(1, len(sizes)):
        qm, km = flat.pop(0), flat.pop(0)
        groups.append((qm, km, flat.pop(0) if step + 1 < len(sizes) else None))
    return groups


def whole_spec():
    return pl.BlockSpec(memory_space=pltpu.VMEM)


def value_spec(length):
    return pl.BlockSpec((length, LEAF), lambda i: (0, 2))


def plain_spec(shape):
    return pl.BlockSpec(shape, lambda i: (0, 0))


def merge_forward_kernel(length, scale, own, v, qm, km, p, lab_col, lab_row, attended, lse, *rest):
    flat, (m_ref, l_ref, o_ref) = rest[:-3], rest[-3:]
    merge_forward(
        length, scale, own, v, qm, km, p, lab_col, lab_row, attended, lse, level_groups(length, flat), m_ref, l_ref, o_ref
    )


def run_merge_forward(proj, own, qm, km, p, lab_col, lab_row, scale):
    length = proj.shape[0]
    extra = level_shapes(length)
    if length > MERGE_LIMIT:
        return long_forward(length, scale, own, proj[:, 2 * LEAF : 3 * LEAF], qm, km, p, lab_row)
    outs = [matrix(length), matrix(length)] + extra
    return pl.pallas_call(
        functools.partial(merge_forward_kernel, length, scale),
        grid=(1,),
        in_specs=[plain_spec(own.shape), value_spec(length)] + [plain_spec(x.shape) for x in (qm, km, p, lab_col, lab_row)],
        out_specs=[plain_spec(x.shape) for x in outs],
        out_shape=outs,
        scratch_shapes=[pltpu.VMEM((length, 1), jnp.float32), pltpu.VMEM((length, 1), jnp.float32), pltpu.VMEM((length, LEAF), jnp.float32)],
        compiler_params=settings(),
        name="merge_forward",
    )(own, proj, qm, km, p, lab_col, lab_row)


def merge_backward_kernel(length, scale, own, v, qm, km, p, *rest):
    count = len(level_shapes(length))
    flat, rest = rest[:count], rest[count:]
    lab_col, lab_row, attended, lse, dout, gown, gqm, gkm, gp, dv, delta_ref = rest[:11]
    levels = [(qm, km, p)] + level_groups(length, flat)
    merge_backward(
        length, scale, own, v, levels, lab_col, lab_row, attended, lse, dout, gown, gqm, gkm, [gp] + list(rest[11:]), dv, delta_ref
    )


def gp_shapes(length):
    return [(length // h * LEAF, LEAF) for h in halves(length)[1:]]


def run_merge_backward(proj, own, qm, km, p, flat, lab_col, lab_row, attended, lse, dout, scale):
    length = proj.shape[0]
    if length > MERGE_LIMIT:
        levels = [(qm, km, p)] + level_groups(length, flat)
        return long_backward(length, scale, own, proj[:, 2 * LEAF : 3 * LEAF], levels, lab_row, attended, lse, dout)
    operands = [own, proj, qm, km, p, *flat, lab_col, lab_row, attended, lse, dout]
    specs = [plain_spec(x.shape) for x in operands]
    specs[1] = value_spec(length)
    return pl.pallas_call(
        functools.partial(merge_backward_kernel, length, scale),
        grid=(1,),
        in_specs=specs,
        out_specs=[plain_spec((length, LEAF))] * 5,
        out_shape=[matrix(length)] * 5,
        scratch_shapes=[pltpu.VMEM((length, 1), jnp.float32)] + [pltpu.VMEM(shape, jnp.float32) for shape in gp_shapes(length)],
        compiler_params=settings(),
        name="merge_backward",
    )(*operands)


SEQ = ("outer", "mid", "core")
INNER = ("mid", "core")
GROUP = ("mid", "core", "head")
EXTRA = 16


def normalize(values):
    return values * lax.rsqrt(jnp.mean(values * values, axis=-1, keepdims=True) + epsilon)


def norm_back(cotangent, normed, values):
    scaled = lax.rsqrt(jnp.mean(values * values, axis=-1, keepdims=True) + epsilon)
    return scaled * (cotangent - normed * jnp.mean(cotangent * normed, axis=-1, keepdims=True))


def dot(a, b, dims=NN):
    return lax.dot_general(a, b, (dims, ((), ())), preferred_element_type=jnp.float32)


def other_head(value):
    return lax.ppermute(value, "head", [(0, 1), (1, 0)])


def by_head(own, other, axis=0):
    first = lax.axis_index("head") == 0
    return jnp.concatenate([jnp.where(first, own, other), jnp.where(first, other, own)], axis=axis)


def padded(value, axis, size):
    widths = [(0, 0)] * value.ndim
    widths[axis] = (0, size - value.shape[axis])
    return jnp.pad(value, widths)


def local(
    tokens, w_query, w_key, w_value, w_house, w_beta, beta_bias, w_out, w_gate, w_up, w_down, gain_attn, gain_mlp, segment_ids, out_grad
):
    low = jnp.bfloat16
    batches, positions, width = tokens.shape
    half = lax.axis_index("head")
    rank = lax.axis_index(SEQ)
    count = lax.axis_size(SEQ)
    inner = lax.axis_size(INNER)
    rows, half_heads = w_beta.shape
    heads = 2 * half_heads
    assert batches == lax.axis_size("head") and heads <= count
    length = count * positions
    units = w_gate.shape[1] // inner
    scale = LEAF ** (-0.5)

    own_tokens = lax.dynamic_index_in_dim(tokens, half, 0, False)
    all_tokens = lax.all_gather(own_tokens, SEQ, axis=0, tiled=True)
    labels = lax.dynamic_index_in_dim(segment_ids, half, 0, False).astype(low)
    by_heads = [w.reshape(rows, half_heads, LEAF) for w in (w_query, w_key, w_value, w_house)]
    packed = jnp.concatenate(by_heads, axis=2).transpose(1, 0, 2)
    beta_row = padded(w_beta.T[:, None, :], 2, 4 * LEAF)
    packed = padded(jnp.concatenate([packed, beta_row], axis=1), 1, rows + EXTRA)
    packed = padded(by_head(packed, other_head(packed)), 0, count)
    label_row = padded(labels[None], 1, 4 * LEAF)[None]
    at_row = lax.broadcasted_iota(jnp.int32, (1, rows + EXTRA, 1), 1) == rows + 1
    packed = jnp.where(at_row, label_row, packed)
    packed = lax.all_to_all(packed, SEQ, 0, 0, tiled=True)
    weight = packed[:, :rows].reshape(width, 4 * LEAF)
    beta_column = padded(packed[:, rows, :rows].reshape(width, 1), 1, LEAF)
    weight = jnp.concatenate([weight, beta_column], axis=1)
    label_all = packed[:, rows + 1, :positions].reshape(1, length).astype(jnp.float32)
    label_column = jnp.broadcast_to(label_all.reshape(length, 1), (length, LEAF))
    bias_all = padded(by_head(beta_bias, other_head(beta_bias)), 0, count)
    bias_row = padded(lax.dynamic_slice(bias_all, (rank,), (1,)), 0, LEAF)
    bias_row = jnp.concatenate([jnp.zeros(4 * LEAF, jnp.float32), bias_row])

    all_inputs = all_tokens.astype(jnp.float32)
    attn_in = (normalize(all_inputs) * gain_attn).astype(low)
    proj = dot(attn_in, weight) + bias_row
    *saved, own_logits, query_moved, key_moved, product = leaf_forward(proj)
    attended, log_total, *levels = run_merge_forward(
        proj, own_logits, query_moved, key_moved, product, label_column, label_all, scale
    )
    attended_low = attended.astype(low)

    blocks = [w.reshape(rows, inner, units) for w in (w_gate, w_up, w_down.T)]
    mlp_weight = jnp.concatenate(blocks, axis=2).transpose(1, 0, 2)
    mlp_weight = lax.all_to_all(mlp_weight, INNER, 0, 0, tiled=True).reshape(inner * rows, 3 * units)
    mlp_weight = lax.all_gather(mlp_weight, "outer", axis=0, tiled=True)
    gate_up_weight, down_weight = mlp_weight[:, : 2 * units], mlp_weight[:, 2 * units :]
    out_own = lax.all_gather(w_out.T, SEQ, axis=0, tiled=True)
    out_other = other_head(out_own)
    grad_group = lax.all_gather(out_grad, INNER, axis=0, tiled=True).reshape(-1, width)

    heads_here = lax.all_to_all(attended_low.reshape(count, positions, LEAF), SEQ, 0, 0, tiled=True)
    heads_here = heads_here[:heads].reshape(2, half_heads, positions, LEAF).transpose(0, 2, 1, 3)
    heads_here = heads_here.reshape(2, positions, half_heads * LEAF)
    branch = dot(lax.dynamic_index_in_dim(heads_here, half, 0, False), out_own, NT)
    branch = branch + dot(lax.dynamic_index_in_dim(heads_here, 1 - half, 0, False), out_other, NT)
    inputs = own_tokens.astype(jnp.float32)
    middle = inputs + branch
    normed_two = normalize(middle)
    mlp_in = (normed_two * gain_mlp).astype(low)

    mlp_group = lax.all_gather(mlp_in, GROUP, axis=0, tiled=True)
    gate_up = dot(mlp_group, gate_up_weight)
    gate, up = gate_up[:, :units], gate_up[:, units:]
    sigmoid_gate = jax.nn.sigmoid(gate)
    silu_gate = gate * sigmoid_gate
    hidden = (silu_gate * up).astype(low)
    hidden_grad = dot(grad_group, down_weight)
    gate_rows = (hidden_grad * up * sigmoid_gate * (1.0 + gate * (1.0 - sigmoid_gate))).astype(low)
    up_rows = (hidden_grad * silu_gate).astype(low)
    rows_grad = jnp.concatenate([gate_rows, up_rows], axis=1)
    mlp_in_part = dot(rows_grad, gate_up_weight, NT).astype(low)
    mlp_in_grad = lax.psum_scatter(mlp_in_part, GROUP, scatter_dimension=0, tiled=True).astype(jnp.float32)
    mlp_part = dot(hidden, down_weight, NT).astype(low)
    mlp_branch = lax.psum_scatter(mlp_part, GROUP, scatter_dimension=0, tiled=True).astype(jnp.float32)
    block_out = (middle + mlp_branch).astype(low)[None]
    block_out = by_head(block_out, other_head(block_out))

    mlp_grads = jnp.concatenate([dot(mlp_group, rows_grad, TN), dot(grad_group, hidden, TN)], axis=1).astype(low)
    mlp_grads = lax.psum_scatter(mlp_grads, "outer", scatter_dimension=0, tiled=True)
    mlp_grads = lax.all_to_all(mlp_grads.reshape(inner, rows, 3 * units), INNER, 0, 0, tiled=True).astype(jnp.float32)
    gate_grad, up_grad, down_grad = (
        mlp_grads[:, :, i * units : (i + 1) * units].transpose(1, 0, 2).reshape(rows, inner * units) for i in range(3)
    )
    down_grad = down_grad.T

    mlp_gain_part = jnp.sum(mlp_in_grad * normed_two, axis=0)
    own_grad = lax.dynamic_index_in_dim(out_grad, half, 0, False).astype(jnp.float32)
    middle_grad = own_grad + norm_back(mlp_in_grad * gain_mlp, normed_two, middle)
    branch_low = middle_grad.astype(low)
    attended_grad = by_head(dot(branch_low, out_own).astype(low)[None], dot(branch_low, out_other).astype(low)[None])
    attended_grad = attended_grad.reshape(2, positions, half_heads, LEAF).transpose(0, 2, 1, 3)
    attended_grad = padded(attended_grad.reshape(heads, positions, LEAF), 0, count)
    attended_grad = lax.all_to_all(attended_grad, SEQ, 0, 0, tiled=True).reshape(length, LEAF).astype(jnp.float32)
    branch_all = lax.all_gather(branch_low, SEQ, axis=0, tiled=True)

    merged = run_merge_backward(
        proj, own_logits, query_moved, key_moved, product, levels, label_column, label_all, attended, log_total, attended_grad, scale
    )
    proj_grad = leaf_backward(proj, saved, merged)

    attn_in_part = dot(proj_grad, weight, NT)
    attn_gain_part = jnp.sum(attn_in_part * normalize(all_inputs), axis=0)
    attn_in_grad = lax.psum_scatter(attn_in_part.astype(low), SEQ, scatter_dimension=0, tiled=True).astype(jnp.float32)

    weight_grad = dot(attn_in, proj_grad, TN)
    out_weight = dot(branch_all, attended_low, TN)
    bias_part = jnp.sum(proj_grad[:, 4 * LEAF :].astype(jnp.float32), axis=0)
    span = 5 * LEAF
    main = jnp.concatenate([weight_grad[:, : 4 * LEAF], out_weight], axis=1).reshape(count, rows, span)
    beta_rows = padded(weight_grad[:, 4 * LEAF].reshape(count, 1, rows), 2, span)
    gains = jnp.concatenate([attn_gain_part, mlp_gain_part]).reshape(-1, 4 * LEAF)
    gain_rows = gains.shape[0]
    small = jnp.concatenate([padded(gains, 1, span), padded(bias_part[None], 1, span)], axis=0)
    small = jnp.broadcast_to(padded(small, 0, EXTRA - 1), (count, EXTRA - 1, span))
    packed_grad = jnp.concatenate([main, beta_rows, small], axis=1).astype(low)
    packed_grad = lax.all_to_all(packed_grad, SEQ, 0, 0, tiled=True)
    gain_sums = jnp.sum(packed_grad[:, rows + 1 : rows + 1 + gain_rows].astype(jnp.float32), axis=0)
    gain_sums = lax.reduce_precision(gain_sums, 8, 7)
    by_half = packed_grad[:heads].reshape(2, half_heads, rows + EXTRA, span)
    kept = lax.dynamic_index_in_dim(by_half, half, 0, False)
    sent = lax.dynamic_index_in_dim(by_half, 1 - half, 0, False)
    sent = sent.at[:, rows + 1 : rows + 1 + gain_rows].set(gain_sums.astype(low)[None])
    came = other_head(sent)
    sums = kept.astype(jnp.float32) + came.astype(jnp.float32)
    gain_sums = gain_sums + came[0, rows + 1 : rows + 1 + gain_rows].astype(jnp.float32)
    gain_sums = gain_sums[:, : 4 * LEAF].reshape(2, width)
    grads = [
        sums[:, :rows, i * LEAF : (i + 1) * LEAF].transpose(1, 0, 2).reshape(rows, half_heads * LEAF) for i in range(4)
    ]
    out_weight_grad = sums[:, :rows, 4 * LEAF :].transpose(0, 2, 1).reshape(half_heads * LEAF, rows)
    beta_grad = sums[:, rows, :rows].T
    bias_grad = sums[:, rows + 1 + gain_rows, 0]

    tokens_grad = (middle_grad + norm_back(attn_in_grad * gain_attn, normalize(inputs), inputs))[None]
    tokens_grad = by_head(tokens_grad, other_head(tokens_grad))
    return (
        block_out, tokens_grad, *grads, beta_grad, bias_grad, out_weight_grad, gate_grad, up_grad, down_grad, gain_sums[0], gain_sums[1]
    )


def solution(mesh):
    inner = (2, 2)
    fine = Mesh(mesh.devices.reshape(-1, *inner, mesh.shape["head"]), (*SEQ, "head"))
    split_rows, split_columns, by_position = P(SEQ, "head"), P("head", SEQ), P(None, SEQ, None)
    placed = (
        (by_position,) + (split_rows,) * 5 + (P("head"), split_columns, split_rows, split_rows, split_columns)
        + (P(), P(), P(None, SEQ), by_position)
    )
    returned = (
        (by_position, by_position) + (split_rows,) * 5 + (P("head"), split_columns, split_rows, split_rows, split_columns, P(), P())
    )
    return jax.shard_map(local, mesh=fine, in_specs=placed, out_specs=returned, check_vma=False)
```

```python
import functools

import jax
import jax.numpy as jnp
from jax import lax
from jax.experimental import pallas as pl
from jax.experimental.pallas import tpu as pltpu
from jax.sharding import Mesh
from jax.sharding import PartitionSpec as P

epsilon = 1e-06
masked_score = -1e30
MERGE_LIMIT = 2048
LEAF = 128
NN, NT, TN = ((1,), (0,)), ((1,), (1,)), ((0,), (0,))


def split(a):
    if isinstance(a, tuple):
        return a
    if a.dtype == jnp.bfloat16:
        return (a, None)
    high = a.astype(jnp.bfloat16)
    return (high, (a - high.astype(jnp.float32)).astype(jnp.bfloat16))


def raw_dot(a, b, dims):
    return lax.dot_general(a, b, (dims, ((), ())), preferred_element_type=jnp.float32)


def dot_parts(a, b, dims):
    (ah, al), (bh, bl) = split(a), split(b)
    total = raw_dot(ah, bh, dims)
    if bl is not None:
        total = total + raw_dot(ah, bl, dims)
    if al is not None:
        total = total + raw_dot(al, bh, dims)
    return total


def grid_of(shape, axis):
    return lax.broadcasted_iota(jnp.int32, shape, axis)


def leaf_masks():
    row, col = grid_of((LEAF, LEAF), 0), grid_of((LEAF, LEAF), 1)
    return row, col


def leaf_forward_kernel(leaves, q_ref, k_ref, h_ref, g_ref, x_out, a_out, c_out, u_out, w_out, tm_out, dots_out, own_out, qm_out, km_out, p_out):
    mm = dot_parts
    row, col = leaf_masks()
    eye = (row == col).astype(jnp.float32)
    span = range(leaves)
    at = [pl.ds(g * LEAF, LEAF) for g in span]
    q = [split(q_ref[i, :]) for i in at]
    k = [split(k_ref[i, :]) for i in at]
    mirror, strength = [], []
    for i in at:
        h = h_ref[i, :]
        mirror.append(split(h * lax.rsqrt(jnp.sum(h * h, axis=-1, keepdims=True) + epsilon)))
        strength.append(2.0 * jax.nn.sigmoid(jnp.broadcast_to(g_ref[i, 0:1], (LEAF, LEAF))))
    dots = [mm(m, m, NT) for m in mirror]
    system = [jnp.where(row > col, d, 0.0) * s for d, s in zip(dots, strength)]
    inverse = [eye - jnp.where((row // 2 == col // 2), n, 0.0) for n in system]
    width = 2
    while width < LEAF:
        picked = (row // (2 * width) == col // (2 * width)) & (row // width != col // width)
        parts = [split(x) for x in inverse]
        off = [split(jnp.where(picked, n, 0.0)) for n in system]
        turned = [mm(x, n, NN) for x, n in zip(parts, off)]
        inverse = [x - mm(t, p, NN) for x, t, p in zip(inverse, turned, parts)]
        width *= 2
    triang = [split(x * s.T) for x, s in zip(inverse, strength)]
    a_part = [split(jnp.where(row >= col, mm(x, m, NT), 0.0)) for x, m in zip(q, mirror)]
    c_part = [split(jnp.where(row < col, mm(x, m, NT), 0.0)) for x, m in zip(k, mirror)]
    own = [mm(x, y, NT) for x, y in zip(q, k)]
    u_part = [split(mm(x, t, NN)) for x, t in zip(a_part, triang)]
    w_part = [split(mm(x, t, NT)) for x, t in zip(c_part, triang)]
    tm_part = [split(mm(t, m, NN)) for t, m in zip(triang, mirror)]
    for g, i in enumerate(at):
        x_out[i, :] = inverse[g]
        dots_out[i, :] = dots[g]
        for ref, value in ((a_out, a_part), (c_out, c_part), (u_out, u_part), (w_out, w_part), (tm_out, tm_part)):
            high, low = value[g]
            ref[i, :] = high.astype(jnp.float32) + low.astype(jnp.float32)
        own_out[i, :] = own[g] - mm(u_part[g], c_part[g], NT)
        qm_out[i, :] = q_ref[i, :] - mm(u_part[g], mirror[g], NN)
        km_out[i, :] = k_ref[i, :] - mm(w_part[g], mirror[g], NN)
        p_out[i, :] = eye - mm(mirror[g], tm_part[g], TN)


def leaf_backward_kernel(leaves, q_ref, k_ref, h_ref, g_ref, x_ref, a_ref, c_ref, u_ref, w_ref, tm_ref, dots_ref, gown_ref, gqm_ref, gkm_ref, gp_ref, dv_ref, out):
    mm = dot_parts
    row, col = leaf_masks()
    ones = jnp.ones((LEAF, LEAF), jnp.bfloat16)
    at = [pl.ds(g * LEAF, LEAF) for g in range(leaves)]
    q = [split(q_ref[i, :]) for i in at]
    k = [split(k_ref[i, :]) for i in at]
    h = [h_ref[i, :] for i in at]
    scaling = [lax.rsqrt(jnp.sum(x * x, axis=-1, keepdims=True) + epsilon) for x in h]
    mirror_full = [x * r for x, r in zip(h, scaling)]
    mirror = [split(x) for x in mirror_full]
    strength = [2.0 * jax.nn.sigmoid(jnp.broadcast_to(g_ref[i, 0:1], (LEAF, LEAF))) for i in at]
    inverse_full = [x_ref[i, :] for i in at]
    inverse = [split(x) for x in inverse_full]
    strength_row = [s.T for s in strength]
    triang = [split(x * s) for x, s in zip(inverse_full, strength_row)]
    a_part = [split(a_ref[i, :]) for i in at]
    c_part = [split(c_ref[i, :]) for i in at]
    u_part = [split(u_ref[i, :]) for i in at]
    w_part = [split(w_ref[i, :]) for i in at]
    tm_part = [split(tm_ref[i, :]) for i in at]
    gown = [split(gown_ref[i, :]) for i in at]
    gqm = [split(gqm_ref[i, :]) for i in at]
    gkm = [split(gkm_ref[i, :]) for i in at]
    gp = [split(gp_ref[i, :]) for i in at]
    span = range(leaves)
    gu = [split(-mm(gqm[g], mirror[g], NT) - mm(gown[g], c_part[g], NN)) for g in span]
    gw = [split(-mm(gkm[g], mirror[g], NT)) for g in span]
    mgp = [split(mm(mirror[g], gp[g], NN)) for g in span]
    ga = [split(jnp.where(row >= col, mm(gu[g], triang[g], NT), 0.0)) for g in span]
    gc = [split(jnp.where(row < col, mm(gw[g], triang[g], NN) - mm(gown[g], u_part[g], TN), 0.0)) for g in span]
    gt = [mm(a_part[g], gu[g], TN) + mm(gw[g], c_part[g], TN) - mm(mgp[g], mirror[g], NT) for g in span]
    gx = [split(gt[g] * strength_row[g]) for g in span]
    xgx = [split(mm(inverse[g], gx[g], TN)) for g in span]
    gn = [jnp.where(row > col, -mm(xgx[g], inverse[g], NT), 0.0) for g in span]
    gdots = [split(strength[g] * gn[g]) for g in span]
    for g, i in enumerate(at):
        gm = (
            -mm(u_part[g], gqm[g], TN)
            - mm(w_part[g], gkm[g], TN)
            + mm(ga[g], q[g], TN)
            + mm(gc[g], k[g], TN)
            + mm(gdots[g], mirror[g], NN)
            + mm(gdots[g], mirror[g], TN)
            - mm(tm_part[g], gp[g], NT)
            - mm(triang[g], mgp[g], TN)
        )
        gq = gqm_ref[i, :] + mm(gown[g], k[g], NN) + mm(ga[g], mirror[g], NN)
        gk = gkm_ref[i, :] + mm(gown[g], q[g], TN) + mm(gc[g], mirror[g], NN)
        gh = scaling[g] * (gm - mirror_full[g] * jnp.sum(gm * mirror_full[g], axis=-1, keepdims=True))
        gs = mm(gn[g] * dots_ref[i, :], ones, NN) + mm(gt[g] * inverse_full[g], ones, TN)
        gl = gs * strength[g] * (1.0 - 0.5 * strength[g])
        out[i, 0:128] = gq.astype(jnp.bfloat16)
        out[i, 128:256] = gk.astype(jnp.bfloat16)
        out[i, 256:384] = dv_ref[i, :].astype(jnp.bfloat16)
        out[i, 384:512] = gh.astype(jnp.bfloat16)
        out[i, 512:640] = jnp.where(col == 0, gl, 0.0).astype(jnp.bfloat16)


def halves(length):
    found, h = [], LEAF
    while h < length:
        found.append(h)
        h *= 2
    return found


def merge_forward(length, scale, own, v, qm, km, p, lab_col, lab_row, attended, lse, levels, m_ref, l_ref, o_ref):
    mm = dot_parts
    row, col = leaf_masks()
    for start in range(0, length, LEAF):
        i = slice(start, start + LEAF)
        allowed = (row >= col) & (lab_col[i, 0:1] == lab_row[:, i])
        scores = jnp.where(allowed, own[i, :] * scale, masked_score)
        top = jnp.max(scores, axis=-1, keepdims=True)
        weights = jnp.exp(scores - top)
        m_ref[i, :] = top
        l_ref[i, :] = jnp.sum(weights, axis=-1, keepdims=True)
        o_ref[i, :] = mm(weights, v[i, :], NN)
    sizes = halves(length)
    for step, h in enumerate(sizes):
        last = step + 1 == len(sizes)
        if not last:
            qm_next, km_next, p_next = levels[step]
        for start in range(0, length, 2 * h):
            a, b = slice(start, start + h), slice(start + h, start + 2 * h)
            pa = slice(start // h * LEAF, start // h * LEAF + LEAF)
            pb = slice(start // h * LEAF + LEAF, start // h * LEAF + 2 * LEAF)
            qm_b, km_a = split(qm[b, :]), split(km[a, :])
            scores = mm(qm_b, km_a, NT) * scale
            scores = jnp.where(lab_col[b, 0:1] == lab_row[:, a], scores, masked_score)
            old = m_ref[b, :]
            top = jnp.maximum(old, jnp.max(scores, axis=-1, keepdims=True))
            factor = jnp.exp(old - top)
            weights = jnp.exp(scores - top)
            m_ref[b, :] = top
            l_ref[b, :] = l_ref[b, :] * factor + jnp.sum(weights, axis=-1, keepdims=True)
            o_ref[b, :] = o_ref[b, :] * factor + mm(weights, v[a, :], NN)
            if not last:
                p_a, p_b = split(p[pa, :]), split(p[pb, :])
                qm_next[a, :] = qm[a, :]
                qm_next[b, :] = mm(qm_b, p_a, NN)
                km_next[b, :] = km[b, :]
                km_next[a, :] = mm(km_a, p_b, NT)
                if p_next is not None:
                    into = start // (2 * h) * LEAF
                    p_next[slice(into, into + LEAF), :] = mm(p_b, p_a, NN)
        if not last:
            qm, km, p = qm_next, km_next, p_next
    total = l_ref[...]
    attended[...] = o_ref[...] / total
    lse[...] = jnp.broadcast_to(m_ref[...] + jnp.log(total), (length, LEAF))


def merge_backward(length, scale, own, v, levels, lab_col, lab_row, attended, lse, dout, gown, gqm, gkm, gp, dv, delta_ref):
    mm = dot_parts
    row, col = leaf_masks()
    delta_ref[...] = jnp.sum(dout[...] * attended[...], axis=-1, keepdims=True)
    for start in range(0, length, LEAF):
        i = slice(start, start + LEAF)
        allowed = (row >= col) & (lab_col[i, 0:1] == lab_row[:, i])
        probs = jnp.where(allowed, jnp.exp(own[i, :] * scale - lse[i, 0:1]), 0.0)
        grad = split(dout[i, :])
        dv[i, :] = mm(probs, grad, TN)
        gown[i, :] = probs * (mm(grad, v[i, :], NT) - delta_ref[i, :]) * scale
    sizes = halves(length)
    for step in reversed(range(len(sizes))):
        h = sizes[step]
        last = step + 1 == len(sizes)
        qm, km, p = levels[step]
        for start in range(0, length, 2 * h):
            a, b = slice(start, start + h), slice(start + h, start + 2 * h)
            pa = slice(start // h * LEAF, start // h * LEAF + LEAF)
            pb = slice(start // h * LEAF + LEAF, start // h * LEAF + 2 * LEAF)
            qm_b, km_a, grad = split(qm[b, :]), split(km[a, :]), split(dout[b, :])
            scores = mm(qm_b, km_a, NT) * scale
            allowed = lab_col[b, 0:1] == lab_row[:, a]
            probs = jnp.where(allowed, jnp.exp(scores - lse[b, 0:1]), 0.0)
            dv[a, :] = dv[a, :] + mm(probs, grad, TN)
            ds = split(probs * (mm(grad, v[a, :], NT) - delta_ref[b, :]) * scale)
            gq_part = mm(ds, km_a, NN)
            gk_part = mm(ds, qm_b, TN)
            if last:
                gqm[a, :] = jnp.zeros((h, LEAF), jnp.float32)
                gkm[b, :] = jnp.zeros((h, LEAF), jnp.float32)
                gqm[b, :] = gq_part
                gkm[a, :] = gk_part
            else:
                p_a, p_b = split(p[pa, :]), split(p[pb, :])
                gq_b, gk_a = split(gqm[b, :]), split(gkm[a, :])
                gp_a, gp_b = mm(qm_b, gq_b, TN), mm(gk_a, km_a, TN)
                if step + 2 < len(sizes):
                    into = start // (2 * h) * LEAF
                    g_up = split(gp[step + 1][slice(into, into + LEAF), :])
                    gp_a, gp_b = gp_a + mm(p_b, g_up, TN), gp_b + mm(g_up, p_a, NT)
                gp[step][pa, :] = gp_a
                gp[step][pb, :] = gp_b
                gqm[b, :] = mm(gq_b, p_a, NT) + gq_part
                gkm[a, :] = mm(gk_a, p_b, NN) + gk_part


def whole_dot(spec, *operands):
    return jnp.einsum(spec, *operands, precision=lax.Precision.HIGHEST)


def pairs(value, size):
    both = value.reshape(-1, 2, size, value.shape[-1])
    return both[:, 0], both[:, 1]


def joined(first, second):
    return jnp.stack([first, second], axis=1).reshape(-1, first.shape[-1])


def long_allowed(label, size, own):
    both = label.reshape(-1, size) if own else label.reshape(-1, 2, size)
    left, right = (both, both) if own else (both[:, 0], both[:, 1])
    same = right[:, :, None] == left[:, None, :]
    return same & jnp.tril(jnp.ones((size, size), jnp.bool_)) if own else same


def long_forward(length, scale, own, v, qm, km, p, label):
    scores = jnp.where(long_allowed(label, LEAF, True), own.reshape(-1, LEAF, LEAF) * scale, masked_score)
    top = jnp.max(scores, axis=-1, keepdims=True)
    weights = jnp.exp(scores - top)
    state = [
        x.reshape(length, -1)
        for x in (top, jnp.sum(weights, axis=-1, keepdims=True), whole_dot("nij,njd->nid", weights, v.reshape(-1, LEAF, LEAF)))
    ]
    levels = []
    for h in halves(length):
        (q_a, q_b), (k_a, k_b), (v_a, _) = pairs(qm, h), pairs(km, h), pairs(v, h)
        scores = whole_dot("nid,njd->nij", q_b, k_a) * scale
        scores = jnp.where(long_allowed(label, h, False), scores, masked_score)
        (m_a, m_b), (l_a, l_b), (o_a, o_b) = (pairs(x, h) for x in state)
        top = jnp.maximum(m_b, jnp.max(scores, axis=-1, keepdims=True))
        factor = jnp.exp(m_b - top)
        weights = jnp.exp(scores - top)
        l_b = l_b * factor + jnp.sum(weights, axis=-1, keepdims=True)
        o_b = o_b * factor + whole_dot("nij,njd->nid", weights, v_a)
        state = [joined(m_a, top), joined(l_a, l_b), joined(o_a, o_b)]
        if 2 * h < length:
            p_a, p_b = pairs(p, LEAF)
            qm = joined(q_a, whole_dot("nid,nde->nie", q_b, p_a))
            km = joined(whole_dot("nid,ned->nie", k_a, p_b), k_b)
            p = whole_dot("nde,nef->ndf", p_b, p_a).reshape(-1, LEAF)
            levels += [qm, km] + ([p] if 4 * h < length else [])
    top, total, out = state
    return [out / total, jnp.broadcast_to(top + jnp.log(total), (length, LEAF))] + levels


def long_backward(length, scale, own, v, levels, label, attended, lse, dout):
    lse = lse[:, :1]
    delta = jnp.sum(dout * attended, axis=-1, keepdims=True)
    blocks = lambda x: x.reshape(length // LEAF, LEAF, -1)
    probs = jnp.exp(blocks(own) * scale - blocks(lse))
    probs = jnp.where(long_allowed(label, LEAF, True), probs, 0.0)
    dv = whole_dot("nij,nid->njd", probs, blocks(dout)).reshape(length, LEAF)
    gown = probs * (whole_dot("nid,njd->nij", blocks(dout), blocks(v)) - blocks(delta)) * scale
    gqm = gkm = gp = None
    for h, (qm, km, p) in reversed(list(zip(halves(length), levels))):
        (_, q_b), (k_a, _), (v_a, _), (_, o_b) = pairs(qm, h), pairs(km, h), pairs(v, h), pairs(dout, h)
        scores = whole_dot("nid,njd->nij", q_b, k_a) * scale - pairs(lse, h)[1]
        probs = jnp.where(long_allowed(label, h, False), jnp.exp(scores), 0.0)
        dv_a, dv_b = pairs(dv, h)
        dv = joined(dv_a + whole_dot("nij,nid->njd", probs, o_b), dv_b)
        ds = probs * (whole_dot("nid,njd->nij", o_b, v_a) - pairs(delta, h)[1]) * scale
        gq_part, gk_part = whole_dot("nij,njd->nid", ds, k_a), whole_dot("nij,nid->njd", ds, q_b)
        if gqm is None:
            gqm, gkm = joined(jnp.zeros_like(gq_part), gq_part), joined(gk_part, jnp.zeros_like(gk_part))
            continue
        (gq_a, gq_b), (gk_a, gk_b), (p_a, p_b) = pairs(gqm, h), pairs(gkm, h), pairs(p, LEAF)
        gp_a, gp_b = whole_dot("nid,nie->nde", q_b, gq_b), whole_dot("nid,nie->nde", gk_a, k_a)
        if gp is not None:
            above = gp.reshape(-1, LEAF, LEAF)
            gp_a = gp_a + whole_dot("nde,ndf->nef", p_b, above)
            gp_b = gp_b + whole_dot("ndf,nef->nde", above, p_a)
        gp = joined(gp_a, gp_b)
        gqm = joined(gq_a, whole_dot("nid,ned->nie", gq_b, p_a) + gq_part)
        gkm = joined(whole_dot("nid,nde->nie", gk_a, p_b) + gk_part, gk_b)
    return [gown.reshape(length, LEAF), gqm, gkm, gp, dv]


def matrix(rows, columns=LEAF, dtype=jnp.float32):
    return jax.ShapeDtypeStruct((rows, columns), dtype)


def cost(flops, moved):
    return pl.CostEstimate(flops=flops, bytes_accessed=moved, transcendentals=0)


def settings():
    return pltpu.CompilerParams(vmem_limit_bytes=56 * 1024 * 1024)


def leaf_group(length):
    leaves = length // LEAF
    return 4 if leaves % 4 == 0 else 1


def leaf_forward(proj):
    length = proj.shape[0]
    leaves = leaf_group(length)
    rows = leaves * LEAF
    column = lambda j: pl.BlockSpec((rows, LEAF), lambda i, j=j: (i, j))
    return pl.pallas_call(
        functools.partial(leaf_forward_kernel, leaves),
        grid=(length // rows,),
        in_specs=[column(0), column(1), column(3), column(4)],
        out_specs=[column(0)] * 11,
        out_shape=[matrix(length)] * 11,
        compiler_params=settings(),
        cost_estimate=cost(1, 1),
        name="leaf_forward",
    )(proj, proj, proj, proj)


def leaf_backward(proj, saved, grads):
    length = proj.shape[0]
    leaves = leaf_group(length)
    rows = leaves * LEAF
    column = lambda j: pl.BlockSpec((rows, LEAF), lambda i, j=j: (i, j))
    return pl.pallas_call(
        functools.partial(leaf_backward_kernel, leaves),
        grid=(length // rows,),
        in_specs=[column(0), column(1), column(3), column(4)] + [column(0)] * (len(saved) + len(grads)),
        out_specs=pl.BlockSpec((rows, 5 * LEAF), lambda i: (i, 0)),
        out_shape=matrix(length, 5 * LEAF, jnp.bfloat16),
        compiler_params=settings(),
        cost_estimate=cost(1, 1),
        name="leaf_backward",
    )(proj, proj, proj, proj, *saved, *grads)


def level_shapes(length):
    sizes = halves(length)
    shapes = []
    for step in range(1, len(sizes)):
        shapes += [matrix(length), matrix(length)]
        if step + 1 < len(sizes):
            shapes.append(matrix(length // sizes[step] * LEAF))
    return shapes


def level_groups(length, flat):
    sizes, groups, flat = halves(length), [], list(flat)
    for step in range(1, len(sizes)):
        qm, km = flat.pop(0), flat.pop(0)
        groups.append((qm, km, flat.pop(0) if step + 1 < len(sizes) else None))
    return groups


def whole_spec():
    return pl.BlockSpec(memory_space=pltpu.VMEM)


def value_spec(length):
    return pl.BlockSpec((length, LEAF), lambda i: (0, 2))


def plain_spec(shape):
    return pl.BlockSpec(shape, lambda i: (0, 0))


def merge_forward_kernel(length, scale, own, v, qm, km, p, lab_col, lab_row, attended, lse, *rest):
    flat, (m_ref, l_ref, o_ref) = rest[:-3], rest[-3:]
    merge_forward(
        length, scale, own, v, qm, km, p, lab_col, lab_row, attended, lse, level_groups(length, flat), m_ref, l_ref, o_ref
    )


def run_merge_forward(proj, own, qm, km, p, lab_col, lab_row, scale):
    length = proj.shape[0]
    extra = level_shapes(length)
    if length > MERGE_LIMIT:
        return long_forward(length, scale, own, proj[:, 2 * LEAF : 3 * LEAF], qm, km, p, lab_row)
    outs = [matrix(length), matrix(length)] + extra
    return pl.pallas_call(
        functools.partial(merge_forward_kernel, length, scale),
        grid=(1,),
        in_specs=[plain_spec(own.shape), value_spec(length)] + [plain_spec(x.shape) for x in (qm, km, p, lab_col, lab_row)],
        out_specs=[plain_spec(x.shape) for x in outs],
        out_shape=outs,
        scratch_shapes=[pltpu.VMEM((length, 1), jnp.float32), pltpu.VMEM((length, 1), jnp.float32), pltpu.VMEM((length, LEAF), jnp.float32)],
        compiler_params=settings(),
        cost_estimate=cost(1, 1),
        name="merge_forward",
    )(own, proj, qm, km, p, lab_col, lab_row)


def merge_backward_kernel(length, scale, own, v, qm, km, p, *rest):
    count = len(level_shapes(length))
    flat, rest = rest[:count], rest[count:]
    lab_col, lab_row, attended, lse, dout, gown, gqm, gkm, gp, dv, delta_ref = rest[:11]
    levels = [(qm, km, p)] + level_groups(length, flat)
    merge_backward(
        length, scale, own, v, levels, lab_col, lab_row, attended, lse, dout, gown, gqm, gkm, [gp] + list(rest[11:]), dv, delta_ref
    )


def gp_shapes(length):
    return [(length // h * LEAF, LEAF) for h in halves(length)[1:]]


def run_merge_backward(proj, own, qm, km, p, flat, lab_col, lab_row, attended, lse, dout, scale):
    length = proj.shape[0]
    if length > MERGE_LIMIT:
        levels = [(qm, km, p)] + level_groups(length, flat)
        return long_backward(length, scale, own, proj[:, 2 * LEAF : 3 * LEAF], levels, lab_row, attended, lse, dout)
    operands = [own, proj, qm, km, p, *flat, lab_col, lab_row, attended, lse, dout]
    specs = [plain_spec(x.shape) for x in operands]
    specs[1] = value_spec(length)
    return pl.pallas_call(
        functools.partial(merge_backward_kernel, length, scale),
        grid=(1,),
        in_specs=specs,
        out_specs=[plain_spec((length, LEAF))] * 5,
        out_shape=[matrix(length)] * 5,
        scratch_shapes=[pltpu.VMEM((length, 1), jnp.float32)] + [pltpu.VMEM(shape, jnp.float32) for shape in gp_shapes(length)],
        compiler_params=settings(),
        cost_estimate=cost(1, 1),
        name="merge_backward",
    )(*operands)


EXTRA = 16


def normalize(values):
    return values * lax.rsqrt(jnp.mean(values * values, axis=-1, keepdims=True) + epsilon)


def norm_back(cotangent, normed, values):
    scaled = lax.rsqrt(jnp.mean(values * values, axis=-1, keepdims=True) + epsilon)
    return scaled * (cotangent - normed * jnp.mean(cotangent * normed, axis=-1, keepdims=True))


def dot(a, b, dims=NN):
    return lax.dot_general(a, b, (dims, ((), ())), preferred_element_type=jnp.float32)


def after(value, *others):
    return lax.optimization_barrier((value, *others))[0]


def swap(value, axis):
    return lax.ppermute(value, axis, [(0, 1), (1, 0)])


def by_index(own, other, axis, at):
    first = lax.axis_index(axis) == 0
    return jnp.stack([jnp.where(first, own, other), jnp.where(first, other, own)], axis=at)


def pick(value, at, index):
    return lax.dynamic_index_in_dim(value, index, at, False)


def gather_at(value, at, axis):
    return by_index(value, swap(value, axis), axis, at)


def gathered(value, axes):
    for at, axis in enumerate(axes):
        value = gather_at(value, at, axis)
    return value


def exchange_at(value, at, axis):
    me = lax.axis_index(axis)
    return by_index(pick(value, at, me), swap(pick(value, at, 1 - me), axis), axis, at)


def exchanged(value, axes):
    for at, axis in enumerate(axes):
        value = exchange_at(value, at, axis)
    return value


def scattered(value, axes):
    for at, axis in reversed(list(enumerate(axes))):
        me = lax.axis_index(axis)
        total = pick(value, at, me).astype(jnp.float32) + swap(pick(value, at, 1 - me), axis).astype(jnp.float32)
        value = total if at == 0 else total.astype(value.dtype)
    return value


def scatter_at(value, at, axis):
    me = lax.axis_index(axis)
    came = swap(pick(value, at, 1 - me), axis).astype(jnp.float32)
    return (pick(value, at, me).astype(jnp.float32) + came).astype(value.dtype)


def copies(value, axes):
    return lax.all_to_all(jnp.broadcast_to(value, (lax.axis_size(axes), *value.shape)), axes, 0, 0, tiled=True)


def sums(value, axes):
    value = value.reshape(lax.axis_size(axes), -1, value.shape[-1])
    return jnp.sum(lax.all_to_all(value, axes, 0, 0, tiled=True).astype(jnp.float32), axis=0)


def padded(value, axis, size):
    widths = [(0, 0)] * value.ndim
    widths[axis] = (0, size - value.shape[axis])
    return jnp.pad(value, widths)


def fence(*values):
    return lax.optimization_barrier(values)


def mlp_kernel(units, cut, act_ref, grad_ref, first_w, second_w, rows_out, hidden_out, part_out):
    act = act_ref[...]
    rest = 2 * units - cut
    first = raw_dot(act, first_w[...], NN)
    second = raw_dot(act, second_w[:, :rest], NN)
    gate = first[:, :units]
    up = jnp.concatenate([first[:, units:], second], axis=1)
    hidden_grad = raw_dot(grad_ref[...], second_w[:, rest:], NN)
    sigmoid_gate = jax.nn.sigmoid(gate)
    silu_gate = gate * sigmoid_gate
    hidden_out[...] = (silu_gate * up).astype(jnp.bfloat16)
    rows_out[:, :units] = (hidden_grad * up * sigmoid_gate * (1.0 + gate * (1.0 - sigmoid_gate))).astype(jnp.bfloat16)
    rows_out[:, units:] = (hidden_grad * silu_gate).astype(jnp.bfloat16)
    part = raw_dot(rows_out[:, :cut], first_w[...], NT) + raw_dot(rows_out[:, cut:], second_w[:, :rest], NT)
    part_out[...] = part.astype(jnp.bfloat16)


def mlp_of(act, grad, first, second):
    tokens, width = act.shape
    units = (first.shape[1] + second.shape[1]) // 3
    outs = [matrix(tokens, 2 * units, jnp.bfloat16), matrix(tokens, units, jnp.bfloat16), matrix(tokens, width, jnp.bfloat16)]
    return pl.pallas_call(
        functools.partial(mlp_kernel, units, first.shape[1]),
        in_specs=[whole_spec()] * 4,
        out_specs=[whole_spec()] * 3,
        out_shape=outs,
        compiler_params=settings(),
        cost_estimate=cost(1, 1),
        name="mlp",
    )(act, grad, first, second)


def mlp_grads_kernel(cuts, act_ref, grad_ref, rows_ref, hidden_ref, first_out, second_out, third_out):
    both = raw_dot(act_ref[...], rows_ref[...], TN).astype(jnp.bfloat16)
    down = raw_dot(grad_ref[...], hidden_ref[...], TN).astype(jnp.bfloat16)
    first_out[...] = both[:, : cuts[0]]
    second_out[...] = both[:, cuts[0] : cuts[1]]
    third_out[:, : both.shape[1] - cuts[1]] = both[:, cuts[1] :]
    third_out[:, both.shape[1] - cuts[1] :] = down


def mlp_grads_of(act, grad, rows, hidden):
    tokens, width = act.shape
    units = hidden.shape[1]
    cuts = (3 * units // 4, 15 * units // 8) if units % (8 * LEAF) == 0 else (3 * units // 4, 7 * units // 4)
    if units % (4 * LEAF):
        cuts = (units, 2 * units)
    widths = (cuts[0], cuts[1] - cuts[0], 3 * units - cuts[1])
    step = 2 * LEAF
    column = pl.BlockSpec((tokens, step), lambda i: (0, i))
    return list(pl.pallas_call(
        functools.partial(mlp_grads_kernel, cuts),
        grid=(width // step,),
        in_specs=[column, column, plain_spec(rows.shape), plain_spec(hidden.shape)],
        out_specs=[pl.BlockSpec((step, w), lambda i: (i, 0)) for w in widths],
        out_shape=[matrix(width, w, jnp.bfloat16) for w in widths],
        compiler_params=settings(),
        cost_estimate=cost(1, 1),
        name="mlp_grads",
    )(act, grad, rows, hidden))


GRAD_ROWS = 3 * LEAF


def pair_grads_kernel(rows, in_ref, grad_ref, weight_ref, gain_ref, out, gain_out):
    result = raw_dot(in_ref[...], grad_ref[...], TN)
    beta = result[:, 4 * LEAF :].T[0:1, :]
    low = result[:, : 4 * LEAF].astype(jnp.bfloat16)
    bias = jnp.sum(grad_ref[:, 4 * LEAF :].astype(jnp.float32), axis=0, keepdims=True)
    wide = lambda x: jnp.concatenate([x, jnp.zeros((1, 4 * LEAF - x.shape[1]), jnp.float32)], axis=1)
    small = jnp.concatenate([wide(beta), wide(bias), jnp.zeros((EXTRA - 2, 4 * LEAF), jnp.float32)], axis=0).astype(jnp.bfloat16)
    for i in range(GRAD_ROWS // rows):
        out[i, :rows, :] = low[i * rows : (i + 1) * rows, :]
        out[i, rows:, :] = small
    products = jnp.sum(result * weight_ref[...].astype(jnp.float32), axis=1, keepdims=True)
    gain_out[...] = jnp.broadcast_to(products, (GRAD_ROWS, LEAF)).T[0:1, :] / gain_ref[...]


def pair_grads_of(attn_in, proj_grad, weight, gain, rows):
    length, width = attn_in.shape
    owners = GRAD_ROWS // rows
    row = pl.BlockSpec((1, GRAD_ROWS), lambda i: (0, i))
    return pl.pallas_call(
        functools.partial(pair_grads_kernel, rows),
        grid=(width // GRAD_ROWS,),
        in_specs=[
            pl.BlockSpec((length, GRAD_ROWS), lambda i: (0, i)),
            plain_spec(proj_grad.shape),
            pl.BlockSpec((GRAD_ROWS, weight.shape[1]), lambda i: (i, 0)),
            row,
        ],
        out_specs=[pl.BlockSpec((owners, rows + EXTRA, 4 * LEAF), lambda i: (i, 0, 0)), row],
        out_shape=[
            jax.ShapeDtypeStruct((width // rows, rows + EXTRA, 4 * LEAF), jnp.bfloat16),
            jax.ShapeDtypeStruct((1, width), jnp.float32),
        ],
        compiler_params=settings(),
        cost_estimate=cost(1, 1),
        name="pair_grads",
    )(attn_in, proj_grad, weight, gain.reshape(1, width))


def local(
    steps, tokens, w_query, w_key, w_value, w_house, w_beta, beta_bias, w_out, w_gate, w_up, w_down, gain_attn, gain_mlp, segment_ids, out_grad
):
    outer_axes, inner_axes = steps[:-2], steps[-2:]
    group = ("head", *inner_axes)
    low = jnp.bfloat16
    batches, positions, width = tokens.shape
    half = lax.axis_index("head")
    rank = lax.axis_index(steps)
    count = lax.axis_size(steps)
    inner = lax.axis_size(inner_axes)
    rows, half_heads = w_beta.shape
    assert batches == lax.axis_size("head") == 2 and 2 * half_heads <= count
    length = count * positions
    units = w_gate.shape[1] // inner
    depth = inner * rows
    scale = LEAF ** (-0.5)
    by_half = lambda own, other, at=0: by_index(own, other, "head", at)

    def gathered_outer(value):
        return lax.all_gather(value, outer_axes, axis=0, tiled=True)

    def to_owner(value):
        return exchanged(value.reshape(2, 2, rows, -1), inner_axes).reshape(inner, rows, -1)

    def outer_sums(value):
        return lax.psum_scatter(value, outer_axes, scatter_dimension=0, tiled=True)

    micro = lax.axis_index(steps[0])
    slots = count // 2
    four = (w_query, w_key, w_value, w_house)
    packed = jnp.stack(
        [jnp.concatenate([w[:, i * LEAF : (i + 1) * LEAF] for w in four], axis=1) for i in range(half_heads)]
    )
    beta_row = padded(w_beta.T[:, None, :], 2, 4 * LEAF)
    label_row = jnp.broadcast_to(padded(segment_ids.astype(low).reshape(1, 1, -1), 2, 4 * LEAF), (half_heads, 1, 4 * LEAF))
    packed = padded(padded(jnp.concatenate([packed, beta_row, label_row], axis=1), 1, rows + EXTRA), 0, slots)
    packed = jnp.broadcast_to(packed[None], (2, *packed.shape)).reshape(count, rows + EXTRA, 4 * LEAF)
    all_tokens = exchanged(tokens, steps[:1])
    blocks = [slice(i * units, (i + 1) * units) for i in range(inner)]
    mlp_own = jnp.stack([jnp.concatenate([w_gate[:, i], w_up[:, i], w_down[i].T], axis=1) for i in blocks])
    mlp_own = exchanged(mlp_own.reshape(2, 2, rows, 3 * units), inner_axes[:1])
    out_own = gathered(w_out.T, steps[:1])
    packed, all_tokens, mlp_own, out_own = fence(packed, all_tokens, mlp_own, out_own)

    packed = lax.all_to_all(packed, steps, 0, 0, tiled=True)
    all_tokens = lax.all_gather(all_tokens, steps[1:], axis=1, tiled=True).reshape(length, width)
    all_inputs = all_tokens.astype(jnp.float32)
    attn_in = (normalize(all_inputs) * gain_attn).astype(low)
    mlp_own = exchange_at(mlp_own, 1, inner_axes[1]).reshape(depth, 3 * units)
    for at in range(1, len(outer_axes)):
        out_own = by_index(out_own, swap(out_own, steps[at]), steps[at], at)
    packed, attn_in, mlp_own, out_own = fence(packed, attn_in, mlp_own, out_own)

    weight = packed[:, :rows].reshape(width, 4 * LEAF)
    beta_column = padded(packed[:, rows, :rows].reshape(width, 1), 1, LEAF)
    weight = jnp.concatenate([weight, beta_column], axis=1)
    label_all = pick(packed[:, rows + 1, : 2 * positions].reshape(count, 2, positions), 1, micro)
    label_all = label_all.reshape(1, length).astype(jnp.float32)
    label_column = jnp.broadcast_to(label_all.reshape(length, 1), (length, LEAF))
    bias_row = padded(lax.dynamic_slice(padded(beta_bias, 0, slots), (rank % slots,), (1,)), 0, LEAF)
    bias_row = jnp.concatenate([jnp.zeros(4 * LEAF, jnp.float32), bias_row])
    cut = 5 * units // 4
    first_weight = gathered_outer(mlp_own[:, :cut])
    proj = dot(attn_in, weight) + bias_row
    proj, out_own, grad_group = fence(proj, out_own, out_grad)

    out_own = gather_at(out_own, len(outer_axes), inner_axes[0])
    *saved, own_logits, query_moved, key_moved, product = leaf_forward(proj)
    own_logits, out_own, grad_group = fence(own_logits, out_own, grad_group)

    out_own = gather_at(out_own, len(outer_axes) + 1, inner_axes[1])
    grad_group = gather_at(grad_group, 1, inner_axes[0])
    attended, log_total, *levels = run_merge_forward(
        proj, own_logits, query_moved, key_moved, product, label_column, label_all, scale
    )
    attended_low = attended.astype(low)
    attended_low, out_own, grad_group, first_weight, mlp_own = fence(attended_low, out_own, grad_group, first_weight, mlp_own)
    out_own = out_own.reshape(width, half_heads * LEAF)

    second_weight = gathered_outer(mlp_own[:, cut:])
    grad_group = gather_at(grad_group, 2, inner_axes[1]).reshape(-1, width)
    heads_here = lax.all_to_all(attended_low.reshape(count, positions, LEAF), steps, 0, 0, tiled=True)
    heads_here = heads_here.reshape(2, slots, positions, LEAF)[:, :half_heads].transpose(0, 2, 1, 3)
    heads_here = heads_here.reshape(2 * positions, half_heads * LEAF)
    branch = dot(heads_here, out_own, NT).reshape(2, positions, width)
    branch = pick(branch, 0, half) + swap(pick(branch, 0, 1 - half), "head")
    inputs = pick(tokens, 0, half).astype(jnp.float32)
    middle = inputs + branch
    normed_two = normalize(middle)
    mlp_in = (normed_two * gain_mlp).astype(low)
    mlp_group = copies(mlp_in, group).reshape(-1, width)
    columns = heads_here.reshape(2 * positions, inner, -1).transpose(1, 0, 2)
    columns = columns.reshape(2, 2, 2 * positions, -1)
    mlp_group, second_weight, grad_group = fence(mlp_group, second_weight, grad_group)

    rows_grad, hidden, mlp_in_part = mlp_of(mlp_group, grad_group, first_weight, second_weight)
    mlp_in_grad = sums(mlp_in_part, group)
    mlp_grads = mlp_grads_of(mlp_group, grad_group, rows_grad, hidden)
    mlp_grads[0] = outer_sums(mlp_grads[0])
    mlp_part = dot(hidden, second_weight[:, 2 * units - cut :], NT).astype(low)
    columns = exchange_at(after(columns, mlp_grads[2]), 0, inner_axes[0])
    mlp_in_grad, mlp_part, columns, *mlp_grads = fence(mlp_in_grad, mlp_part, columns, *mlp_grads)

    mlp_grads[1] = outer_sums(mlp_grads[1])
    mlp_grads[0] = to_owner(mlp_grads[0])
    mlp_part = scattered(mlp_part.reshape(2, 2, 2, positions, width), ("head",)).astype(low)
    mlp_gain_part = jnp.sum(mlp_in_grad * normed_two, axis=0)
    own_grad = pick(out_grad, 0, half).astype(jnp.float32)
    middle_grad = own_grad + norm_back(mlp_in_grad * gain_mlp, normed_two, middle)
    branch_low = middle_grad.astype(low)
    branch_low = by_half(branch_low, swap(branch_low, "head"))
    attended_grad = dot(branch_low.reshape(2 * positions, width), out_own).astype(low)
    attended_grad = attended_grad.reshape(2, positions, half_heads, LEAF).transpose(0, 2, 1, 3)
    attended_grad = padded(attended_grad, 1, slots).reshape(count, positions, LEAF)
    attended_grad = lax.all_to_all(attended_grad, steps, 0, 0, tiled=True).reshape(length, LEAF).astype(jnp.float32)
    branch_group = gather_at(gather_at(branch_low, 1, inner_axes[0]), 2, inner_axes[1]).reshape(-1, width)
    columns = exchange_at(columns, 1, inner_axes[1]).reshape(inner, 2, positions, -1)
    columns = columns.swapaxes(0, 1).reshape(-1, columns.shape[-1])
    attended_grad, branch_group, columns, mlp_part, *mlp_grads = fence(attended_grad, branch_group, columns, mlp_part, *mlp_grads)

    mlp_grads[2] = outer_sums(mlp_grads[2])
    mlp_grads[1] = exchange_at(mlp_grads[1].reshape(2, 2, rows, -1), 0, inner_axes[0])
    mlp_part = scattered(mlp_part.swapaxes(0, 1), inner_axes[1:]).astype(low)
    out_weight_grad = dot(branch_group, columns, TN).astype(low).reshape(count, rows, -1)
    attended_grad = after(attended_grad, out_weight_grad)
    out_weight_grad = lax.all_to_all(out_weight_grad, steps, 0, 0, tiled=True)
    merged = run_merge_backward(
        proj, own_logits, query_moved, key_moved, product, levels, label_column, label_all, attended, log_total, attended_grad, scale
    )
    mlp_part, mlp_grads[1], *merged = fence(mlp_part, mlp_grads[1], *merged)

    mlp_grads[1] = exchange_at(mlp_grads[1], 1, inner_axes[1]).reshape(inner, rows, -1)
    mlp_part = scattered(mlp_part, inner_axes[:1])
    proj_grad = leaf_backward(proj, saved, merged)
    proj_grad, mlp_part, out_weight_grad, *mlp_grads = fence(proj_grad, mlp_part, out_weight_grad, *mlp_grads)

    packed_grad, attn_gain_part = pair_grads_of(attn_in, proj_grad, weight, gain_attn, rows)
    attn_in_part = dot(after(proj_grad, packed_grad), weight, NT)
    packed_grad = lax.all_to_all(packed_grad, steps, 0, 0, tiled=True)
    attn_in_part = attn_in_part.astype(low).reshape(2, *(2,) * (len(steps) - 1), positions, width)
    for at in range(len(steps) - 1, 0, -1):
        attn_in_part = scatter_at(attn_in_part, at, steps[at])
        if at == len(outer_axes):
            mlp_grads[2] = after(mlp_grads[2], attn_in_part)
    attn_in_part = exchanged(attn_in_part, steps[:1])
    attn_in_grad = scattered(attn_in_part, ("head",))

    block_out = (middle + mlp_part).astype(low)
    block_out = by_half(block_out, swap(block_out, "head"))
    mlp_grads[2] = to_owner(mlp_grads[2])
    mlp_grads = jnp.concatenate(mlp_grads, axis=2).astype(jnp.float32)
    gate_grad, up_grad = (
        mlp_grads[:, :, i * units : (i + 1) * units].transpose(1, 0, 2).reshape(rows, inner * units) for i in range(2)
    )
    down_grad = mlp_grads[:, :, 2 * units :].transpose(0, 2, 1).reshape(inner * units, rows)
    out_weight_grad = jnp.sum(out_weight_grad.reshape(-1, inner, rows, out_weight_grad.shape[-1]).astype(jnp.float32), axis=0)
    out_weight_grad = out_weight_grad.transpose(0, 2, 1).reshape(-1, rows)

    gains = jnp.stack([attn_gain_part[0], mlp_gain_part])
    gains = after(gains, packed_grad)
    for axis in (*steps, "head"):
        gains = gains + swap(gains, axis)
    small = after(packed_grad[:, rows : rows + 2], gains)
    small = jnp.sum(small.reshape(2, slots, 2, -1)[:, :half_heads].astype(jnp.float32), axis=0)
    turn = rank % (GRAD_ROWS // rows) * rows
    beta_grad = lax.dynamic_slice(small[:, 0], (0, turn), (half_heads, rows)).T
    bias_grad = small[:, 1, 0]
    total = packed_grad[:, :rows].reshape(2, slots, rows, -1)[:, :half_heads].astype(jnp.float32)
    total = total[0] + total[1]
    grads = [total[..., i * LEAF : (i + 1) * LEAF].transpose(1, 0, 2).reshape(rows, half_heads * LEAF) for i in range(4)]

    tokens_grad = middle_grad + norm_back(attn_in_grad * gain_attn, normalize(inputs), inputs)
    tokens_grad = by_half(tokens_grad, swap(tokens_grad, "head"))
    return (
        block_out, tokens_grad, *grads, beta_grad, bias_grad, out_weight_grad, gate_grad, up_grad, down_grad, gains[0], gains[1]
    )


def solution(mesh):
    depth = mesh.shape["seq"].bit_length() - 1
    assert mesh.shape["seq"] == 2**depth and mesh.shape["head"] == 2
    steps = tuple(f"s{i}" for i in range(depth))
    fine = Mesh(mesh.devices.reshape(*(2,) * depth, 2), (*steps, "head"))
    split_rows, split_columns, by_position = P(steps, "head"), P("head", steps), P(None, steps, None)
    placed = (
        (by_position,) + (split_rows,) * 5 + (P("head"), split_columns, split_rows, split_rows, split_columns)
        + (P(), P(), P(None, steps), by_position)
    )
    returned = (
        (by_position, by_position) + (split_rows,) * 5 + (P("head"), split_columns, split_rows, split_rows, split_columns, P(), P())
    )
    return jax.shard_map(functools.partial(local, steps), mesh=fine, in_specs=placed, out_specs=returned, check_vma=False)
```

```python
import functools

import jax
import jax.numpy as jnp
from jax import lax
from jax.experimental import pallas as pl
from jax.experimental.pallas import tpu as pltpu
from jax.sharding import Mesh
from jax.sharding import PartitionSpec as P

epsilon = 1e-06
masked_score = -1e30
MERGE_LIMIT = 2048
LEAF = 128
NN, NT, TN = ((1,), (0,)), ((1,), (1,)), ((0,), (0,))


def split(a):
    if isinstance(a, tuple):
        return a
    if a.dtype == jnp.bfloat16:
        return (a, None)
    high = a.astype(jnp.bfloat16)
    return (high, (a - high.astype(jnp.float32)).astype(jnp.bfloat16))


def raw_dot(a, b, dims):
    return lax.dot_general(a, b, (dims, ((), ())), preferred_element_type=jnp.float32)


def dot_parts(a, b, dims):
    (ah, al), (bh, bl) = split(a), split(b)
    total = raw_dot(ah, bh, dims)
    if bl is not None:
        total = total + raw_dot(ah, bl, dims)
    if al is not None:
        total = total + raw_dot(al, bh, dims)
    return total


def grid_of(shape, axis):
    return lax.broadcasted_iota(jnp.int32, shape, axis)


def leaf_masks():
    row, col = grid_of((LEAF, LEAF), 0), grid_of((LEAF, LEAF), 1)
    return row, col


def leaf_forward_kernel(leaves, q_ref, k_ref, h_ref, g_ref, x_out, a_out, c_out, u_out, w_out, tm_out, dots_out, own_out, qm_out, km_out, p_out):
    mm = dot_parts
    row, col = leaf_masks()
    eye = (row == col).astype(jnp.float32)
    span = range(leaves)
    at = [pl.ds(g * LEAF, LEAF) for g in span]
    q = [split(q_ref[i, :]) for i in at]
    k = [split(k_ref[i, :]) for i in at]
    mirror, strength = [], []
    for i in at:
        h = h_ref[i, :]
        mirror.append(split(h * lax.rsqrt(jnp.sum(h * h, axis=-1, keepdims=True) + epsilon)))
        strength.append(2.0 * jax.nn.sigmoid(jnp.broadcast_to(g_ref[i, 0:1], (LEAF, LEAF))))
    dots = [mm(m, m, NT) for m in mirror]
    system = [jnp.where(row > col, d, 0.0) * s for d, s in zip(dots, strength)]
    inverse = [eye - jnp.where((row // 2 == col // 2), n, 0.0) for n in system]
    width = 2
    while width < LEAF:
        picked = (row // (2 * width) == col // (2 * width)) & (row // width != col // width)
        parts = [split(x) for x in inverse]
        off = [split(jnp.where(picked, n, 0.0)) for n in system]
        turned = [mm(x, n, NN) for x, n in zip(parts, off)]
        inverse = [x - mm(t, p, NN) for x, t, p in zip(inverse, turned, parts)]
        width *= 2
    triang = [split(x * s.T) for x, s in zip(inverse, strength)]
    a_part = [split(jnp.where(row >= col, mm(x, m, NT), 0.0)) for x, m in zip(q, mirror)]
    c_part = [split(jnp.where(row < col, mm(x, m, NT), 0.0)) for x, m in zip(k, mirror)]
    own = [mm(x, y, NT) for x, y in zip(q, k)]
    u_part = [split(mm(x, t, NN)) for x, t in zip(a_part, triang)]
    w_part = [split(mm(x, t, NT)) for x, t in zip(c_part, triang)]
    tm_part = [split(mm(t, m, NN)) for t, m in zip(triang, mirror)]
    for g, i in enumerate(at):
        x_out[i, :] = inverse[g]
        dots_out[i, :] = dots[g]
        for ref, value in ((a_out, a_part), (c_out, c_part), (u_out, u_part), (w_out, w_part), (tm_out, tm_part)):
            high, low = value[g]
            ref[i, :] = high.astype(jnp.float32) + low.astype(jnp.float32)
        own_out[i, :] = own[g] - mm(u_part[g], c_part[g], NT)
        qm_out[i, :] = q_ref[i, :] - mm(u_part[g], mirror[g], NN)
        km_out[i, :] = k_ref[i, :] - mm(w_part[g], mirror[g], NN)
        p_out[i, :] = eye - mm(mirror[g], tm_part[g], TN)


def leaf_backward_kernel(leaves, q_ref, k_ref, h_ref, g_ref, x_ref, a_ref, c_ref, u_ref, w_ref, tm_ref, dots_ref, gown_ref, gqm_ref, gkm_ref, gp_ref, dv_ref, out):
    mm = dot_parts
    row, col = leaf_masks()
    ones = jnp.ones((LEAF, LEAF), jnp.bfloat16)
    at = [pl.ds(g * LEAF, LEAF) for g in range(leaves)]
    q = [split(q_ref[i, :]) for i in at]
    k = [split(k_ref[i, :]) for i in at]
    h = [h_ref[i, :] for i in at]
    scaling = [lax.rsqrt(jnp.sum(x * x, axis=-1, keepdims=True) + epsilon) for x in h]
    mirror_full = [x * r for x, r in zip(h, scaling)]
    mirror = [split(x) for x in mirror_full]
    strength = [2.0 * jax.nn.sigmoid(jnp.broadcast_to(g_ref[i, 0:1], (LEAF, LEAF))) for i in at]
    inverse_full = [x_ref[i, :] for i in at]
    inverse = [split(x) for x in inverse_full]
    strength_row = [s.T for s in strength]
    triang = [split(x * s) for x, s in zip(inverse_full, strength_row)]
    a_part = [split(a_ref[i, :]) for i in at]
    c_part = [split(c_ref[i, :]) for i in at]
    u_part = [split(u_ref[i, :]) for i in at]
    w_part = [split(w_ref[i, :]) for i in at]
    tm_part = [split(tm_ref[i, :]) for i in at]
    gown = [split(gown_ref[i, :]) for i in at]
    gqm = [split(gqm_ref[i, :]) for i in at]
    gkm = [split(gkm_ref[i, :]) for i in at]
    gp = [split(gp_ref[i, :]) for i in at]
    span = range(leaves)
    gu = [split(-mm(gqm[g], mirror[g], NT) - mm(gown[g], c_part[g], NN)) for g in span]
    gw = [split(-mm(gkm[g], mirror[g], NT)) for g in span]
    mgp = [split(mm(mirror[g], gp[g], NN)) for g in span]
    ga = [split(jnp.where(row >= col, mm(gu[g], triang[g], NT), 0.0)) for g in span]
    gc = [split(jnp.where(row < col, mm(gw[g], triang[g], NN) - mm(gown[g], u_part[g], TN), 0.0)) for g in span]
    gt = [mm(a_part[g], gu[g], TN) + mm(gw[g], c_part[g], TN) - mm(mgp[g], mirror[g], NT) for g in span]
    gx = [split(gt[g] * strength_row[g]) for g in span]
    xgx = [split(mm(inverse[g], gx[g], TN)) for g in span]
    gn = [jnp.where(row > col, -mm(xgx[g], inverse[g], NT), 0.0) for g in span]
    gdots = [split(strength[g] * gn[g]) for g in span]
    for g, i in enumerate(at):
        gm = (
            -mm(u_part[g], gqm[g], TN)
            - mm(w_part[g], gkm[g], TN)
            + mm(ga[g], q[g], TN)
            + mm(gc[g], k[g], TN)
            + mm(gdots[g], mirror[g], NN)
            + mm(gdots[g], mirror[g], TN)
            - mm(tm_part[g], gp[g], NT)
            - mm(triang[g], mgp[g], TN)
        )
        gq = gqm_ref[i, :] + mm(gown[g], k[g], NN) + mm(ga[g], mirror[g], NN)
        gk = gkm_ref[i, :] + mm(gown[g], q[g], TN) + mm(gc[g], mirror[g], NN)
        gh = scaling[g] * (gm - mirror_full[g] * jnp.sum(gm * mirror_full[g], axis=-1, keepdims=True))
        gs = mm(gn[g] * dots_ref[i, :], ones, NN) + mm(gt[g] * inverse_full[g], ones, TN)
        gl = gs * strength[g] * (1.0 - 0.5 * strength[g])
        out[i, 0:128] = gq.astype(jnp.bfloat16)
        out[i, 128:256] = gk.astype(jnp.bfloat16)
        out[i, 256:384] = dv_ref[i, :].astype(jnp.bfloat16)
        out[i, 384:512] = gh.astype(jnp.bfloat16)
        out[i, 512:640] = jnp.where(col == 0, gl, 0.0).astype(jnp.bfloat16)


def halves(length):
    found, h = [], LEAF
    while h < length:
        found.append(h)
        h *= 2
    return found


def merge_forward(length, scale, own, v, qm, km, p, lab_col, lab_row, attended, attended_low, lse, levels, m_ref, l_ref, o_ref):
    mm = dot_parts
    row, col = leaf_masks()
    for start in range(0, length, LEAF):
        i = slice(start, start + LEAF)
        allowed = (row >= col) & (lab_col[i, 0:1] == lab_row[:, i])
        scores = jnp.where(allowed, own[i, :] * scale, masked_score)
        top = jnp.max(scores, axis=-1, keepdims=True)
        weights = jnp.exp(scores - top)
        m_ref[i, :] = top
        l_ref[i, :] = jnp.sum(weights, axis=-1, keepdims=True)
        o_ref[i, :] = mm(weights, v[i, :], NN)
    sizes = halves(length)
    for step, h in enumerate(sizes):
        last = step + 1 == len(sizes)
        if not last:
            qm_next, km_next, p_next = levels[step]
        for start in range(0, length, 2 * h):
            a, b = slice(start, start + h), slice(start + h, start + 2 * h)
            pa = slice(start // h * LEAF, start // h * LEAF + LEAF)
            pb = slice(start // h * LEAF + LEAF, start // h * LEAF + 2 * LEAF)
            qm_b, km_a = split(qm[b, :]), split(km[a, :])
            scores = mm(qm_b, km_a, NT) * scale
            scores = jnp.where(lab_col[b, 0:1] == lab_row[:, a], scores, masked_score)
            old = m_ref[b, :]
            top = jnp.maximum(old, jnp.max(scores, axis=-1, keepdims=True))
            factor = jnp.exp(old - top)
            weights = jnp.exp(scores - top)
            m_ref[b, :] = top
            l_ref[b, :] = l_ref[b, :] * factor + jnp.sum(weights, axis=-1, keepdims=True)
            o_ref[b, :] = o_ref[b, :] * factor + mm(weights, v[a, :], NN)
            if not last:
                p_a, p_b = split(p[pa, :]), split(p[pb, :])
                qm_next[a, :] = qm[a, :]
                qm_next[b, :] = mm(qm_b, p_a, NN)
                km_next[b, :] = km[b, :]
                km_next[a, :] = mm(km_a, p_b, NT)
                if p_next is not None:
                    into = start // (2 * h) * LEAF
                    p_next[slice(into, into + LEAF), :] = mm(p_b, p_a, NN)
        if not last:
            qm, km, p = qm_next, km_next, p_next
    total = l_ref[...]
    result = o_ref[...] / total
    attended[...] = result
    attended_low[...] = result.astype(jnp.bfloat16)
    lse[...] = jnp.broadcast_to(m_ref[...] + jnp.log(total), (length, LEAF))


def merge_backward(length, scale, own, v, levels, lab_col, lab_row, attended, lse, dout, gown, gqm, gkm, gp, dv, delta_ref):
    mm = dot_parts
    row, col = leaf_masks()
    delta_ref[...] = jnp.sum(dout[...] * attended[...], axis=-1, keepdims=True)
    for start in range(0, length, LEAF):
        i = slice(start, start + LEAF)
        allowed = (row >= col) & (lab_col[i, 0:1] == lab_row[:, i])
        probs = jnp.where(allowed, jnp.exp(own[i, :] * scale - lse[i, 0:1]), 0.0)
        grad = split(dout[i, :])
        dv[i, :] = mm(probs, grad, TN)
        gown[i, :] = probs * (mm(grad, v[i, :], NT) - delta_ref[i, :]) * scale
    sizes = halves(length)
    for step in reversed(range(len(sizes))):
        h = sizes[step]
        last = step + 1 == len(sizes)
        qm, km, p = levels[step]
        for start in range(0, length, 2 * h):
            a, b = slice(start, start + h), slice(start + h, start + 2 * h)
            pa = slice(start // h * LEAF, start // h * LEAF + LEAF)
            pb = slice(start // h * LEAF + LEAF, start // h * LEAF + 2 * LEAF)
            qm_b, km_a, grad = split(qm[b, :]), split(km[a, :]), split(dout[b, :])
            scores = mm(qm_b, km_a, NT) * scale
            allowed = lab_col[b, 0:1] == lab_row[:, a]
            probs = jnp.where(allowed, jnp.exp(scores - lse[b, 0:1]), 0.0)
            dv[a, :] = dv[a, :] + mm(probs, grad, TN)
            ds = split(probs * (mm(grad, v[a, :], NT) - delta_ref[b, :]) * scale)
            gq_part = mm(ds, km_a, NN)
            gk_part = mm(ds, qm_b, TN)
            if last:
                gqm[a, :] = jnp.zeros((h, LEAF), jnp.float32)
                gkm[b, :] = jnp.zeros((h, LEAF), jnp.float32)
                gqm[b, :] = gq_part
                gkm[a, :] = gk_part
            else:
                p_a, p_b = split(p[pa, :]), split(p[pb, :])
                gq_b, gk_a = split(gqm[b, :]), split(gkm[a, :])
                gp_a, gp_b = mm(qm_b, gq_b, TN), mm(gk_a, km_a, TN)
                if step + 2 < len(sizes):
                    into = start // (2 * h) * LEAF
                    g_up = split(gp[step + 1][slice(into, into + LEAF), :])
                    gp_a, gp_b = gp_a + mm(p_b, g_up, TN), gp_b + mm(g_up, p_a, NT)
                gp[step][pa, :] = gp_a
                gp[step][pb, :] = gp_b
                gqm[b, :] = mm(gq_b, p_a, NT) + gq_part
                gkm[a, :] = mm(gk_a, p_b, NN) + gk_part


def whole_dot(spec, *operands):
    return jnp.einsum(spec, *operands, precision=lax.Precision.HIGHEST)


def pairs(value, size):
    both = value.reshape(-1, 2, size, value.shape[-1])
    return both[:, 0], both[:, 1]


def joined(first, second):
    return jnp.stack([first, second], axis=1).reshape(-1, first.shape[-1])


def long_allowed(label, size, own):
    both = label.reshape(-1, size) if own else label.reshape(-1, 2, size)
    left, right = (both, both) if own else (both[:, 0], both[:, 1])
    same = right[:, :, None] == left[:, None, :]
    return same & jnp.tril(jnp.ones((size, size), jnp.bool_)) if own else same


def long_forward(length, scale, own, v, qm, km, p, label):
    scores = jnp.where(long_allowed(label, LEAF, True), own.reshape(-1, LEAF, LEAF) * scale, masked_score)
    top = jnp.max(scores, axis=-1, keepdims=True)
    weights = jnp.exp(scores - top)
    state = [
        x.reshape(length, -1)
        for x in (top, jnp.sum(weights, axis=-1, keepdims=True), whole_dot("nij,njd->nid", weights, v.reshape(-1, LEAF, LEAF)))
    ]
    levels = []
    for h in halves(length):
        (q_a, q_b), (k_a, k_b), (v_a, _) = pairs(qm, h), pairs(km, h), pairs(v, h)
        scores = whole_dot("nid,njd->nij", q_b, k_a) * scale
        scores = jnp.where(long_allowed(label, h, False), scores, masked_score)
        (m_a, m_b), (l_a, l_b), (o_a, o_b) = (pairs(x, h) for x in state)
        top = jnp.maximum(m_b, jnp.max(scores, axis=-1, keepdims=True))
        factor = jnp.exp(m_b - top)
        weights = jnp.exp(scores - top)
        l_b = l_b * factor + jnp.sum(weights, axis=-1, keepdims=True)
        o_b = o_b * factor + whole_dot("nij,njd->nid", weights, v_a)
        state = [joined(m_a, top), joined(l_a, l_b), joined(o_a, o_b)]
        if 2 * h < length:
            p_a, p_b = pairs(p, LEAF)
            qm = joined(q_a, whole_dot("nid,nde->nie", q_b, p_a))
            km = joined(whole_dot("nid,ned->nie", k_a, p_b), k_b)
            p = whole_dot("nde,nef->ndf", p_b, p_a).reshape(-1, LEAF)
            levels += [qm, km] + ([p] if 4 * h < length else [])
    top, total, out = state
    return [out / total, (out / total).astype(jnp.bfloat16), jnp.broadcast_to(top + jnp.log(total), (length, LEAF))] + levels


def long_backward(length, scale, own, v, levels, label, attended, lse, dout):
    lse = lse[:, :1]
    delta = jnp.sum(dout * attended, axis=-1, keepdims=True)
    blocks = lambda x: x.reshape(length // LEAF, LEAF, -1)
    probs = jnp.exp(blocks(own) * scale - blocks(lse))
    probs = jnp.where(long_allowed(label, LEAF, True), probs, 0.0)
    dv = whole_dot("nij,nid->njd", probs, blocks(dout)).reshape(length, LEAF)
    gown = probs * (whole_dot("nid,njd->nij", blocks(dout), blocks(v)) - blocks(delta)) * scale
    gqm = gkm = gp = None
    for h, (qm, km, p) in reversed(list(zip(halves(length), levels))):
        (_, q_b), (k_a, _), (v_a, _), (_, o_b) = pairs(qm, h), pairs(km, h), pairs(v, h), pairs(dout, h)
        scores = whole_dot("nid,njd->nij", q_b, k_a) * scale - pairs(lse, h)[1]
        probs = jnp.where(long_allowed(label, h, False), jnp.exp(scores), 0.0)
        dv_a, dv_b = pairs(dv, h)
        dv = joined(dv_a + whole_dot("nij,nid->njd", probs, o_b), dv_b)
        ds = probs * (whole_dot("nid,njd->nij", o_b, v_a) - pairs(delta, h)[1]) * scale
        gq_part, gk_part = whole_dot("nij,njd->nid", ds, k_a), whole_dot("nij,nid->njd", ds, q_b)
        if gqm is None:
            gqm, gkm = joined(jnp.zeros_like(gq_part), gq_part), joined(gk_part, jnp.zeros_like(gk_part))
            continue
        (gq_a, gq_b), (gk_a, gk_b), (p_a, p_b) = pairs(gqm, h), pairs(gkm, h), pairs(p, LEAF)
        gp_a, gp_b = whole_dot("nid,nie->nde", q_b, gq_b), whole_dot("nid,nie->nde", gk_a, k_a)
        if gp is not None:
            above = gp.reshape(-1, LEAF, LEAF)
            gp_a = gp_a + whole_dot("nde,ndf->nef", p_b, above)
            gp_b = gp_b + whole_dot("ndf,nef->nde", above, p_a)
        gp = joined(gp_a, gp_b)
        gqm = joined(gq_a, whole_dot("nid,ned->nie", gq_b, p_a) + gq_part)
        gkm = joined(whole_dot("nid,nde->nie", gk_a, p_b) + gk_part, gk_b)
    return [gown.reshape(length, LEAF), gqm, gkm, gp, dv]


def matrix(rows, columns=LEAF, dtype=jnp.float32):
    return jax.ShapeDtypeStruct((rows, columns), dtype)


def cost(flops, moved):
    return pl.CostEstimate(flops=flops, bytes_accessed=moved, transcendentals=0)


def settings():
    return pltpu.CompilerParams(vmem_limit_bytes=56 * 1024 * 1024)


def leaf_group(length):
    leaves = length // LEAF
    return 4 if leaves % 4 == 0 else 1


def leaf_forward(proj):
    length = proj.shape[0]
    leaves = leaf_group(length)
    rows = leaves * LEAF
    column = lambda j: pl.BlockSpec((rows, LEAF), lambda i, j=j: (i, j))
    return pl.pallas_call(
        functools.partial(leaf_forward_kernel, leaves),
        grid=(length // rows,),
        in_specs=[column(0), column(1), column(3), column(4)],
        out_specs=[column(0)] * 11,
        out_shape=[matrix(length)] * 11,
        compiler_params=settings(),
        cost_estimate=cost(1, 1),
        name="leaf_forward",
    )(proj, proj, proj, proj)


def leaf_backward(proj, saved, grads):
    length = proj.shape[0]
    leaves = leaf_group(length)
    rows = leaves * LEAF
    column = lambda j: pl.BlockSpec((rows, LEAF), lambda i, j=j: (i, j))
    return pl.pallas_call(
        functools.partial(leaf_backward_kernel, leaves),
        grid=(length // rows,),
        in_specs=[column(0), column(1), column(3), column(4)] + [column(0)] * (len(saved) + len(grads)),
        out_specs=pl.BlockSpec((rows, 5 * LEAF), lambda i: (i, 0)),
        out_shape=matrix(length, 5 * LEAF, jnp.bfloat16),
        compiler_params=settings(),
        cost_estimate=cost(1, 1),
        name="leaf_backward",
    )(proj, proj, proj, proj, *saved, *grads)


def level_shapes(length):
    sizes = halves(length)
    shapes = []
    for step in range(1, len(sizes)):
        shapes += [matrix(length), matrix(length)]
        if step + 1 < len(sizes):
            shapes.append(matrix(length // sizes[step] * LEAF))
    return shapes


def level_groups(length, flat):
    sizes, groups, flat = halves(length), [], list(flat)
    for step in range(1, len(sizes)):
        qm, km = flat.pop(0), flat.pop(0)
        groups.append((qm, km, flat.pop(0) if step + 1 < len(sizes) else None))
    return groups


def whole_spec():
    return pl.BlockSpec(memory_space=pltpu.VMEM)


def value_spec(length):
    return pl.BlockSpec((length, LEAF), lambda i: (0, 2))


def plain_spec(shape):
    return pl.BlockSpec(shape, lambda i: (0, 0))


def merge_forward_kernel(length, scale, own, v, qm, km, p, lab_col, lab_row, attended, attended_low, lse, *rest):
    flat, (m_ref, l_ref, o_ref) = rest[:-3], rest[-3:]
    merge_forward(
        length, scale, own, v, qm, km, p, lab_col, lab_row, attended, attended_low, lse, level_groups(length, flat), m_ref, l_ref, o_ref
    )


def run_merge_forward(proj, own, qm, km, p, lab_col, lab_row, scale):
    length = proj.shape[0]
    extra = level_shapes(length)
    if length > MERGE_LIMIT:
        return long_forward(length, scale, own, proj[:, 2 * LEAF : 3 * LEAF], qm, km, p, lab_row)
    outs = [matrix(length), matrix(length, LEAF, jnp.bfloat16), matrix(length)] + extra
    return pl.pallas_call(
        functools.partial(merge_forward_kernel, length, scale),
        grid=(1,),
        in_specs=[plain_spec(own.shape), value_spec(length)] + [plain_spec(x.shape) for x in (qm, km, p, lab_col, lab_row)],
        out_specs=[plain_spec(x.shape) for x in outs],
        out_shape=outs,
        scratch_shapes=[pltpu.VMEM((length, 1), jnp.float32), pltpu.VMEM((length, 1), jnp.float32), pltpu.VMEM((length, LEAF), jnp.float32)],
        compiler_params=settings(),
        cost_estimate=cost(1, 1),
        name="merge_forward",
    )(own, proj, qm, km, p, lab_col, lab_row)


def merge_backward_kernel(length, scale, own, v, qm, km, p, *rest):
    count = len(level_shapes(length))
    flat, rest = rest[:count], rest[count:]
    lab_col, lab_row, attended, lse, dout, gown, gqm, gkm, gp, dv, delta_ref = rest[:11]
    levels = [(qm, km, p)] + level_groups(length, flat)
    merge_backward(
        length, scale, own, v, levels, lab_col, lab_row, attended, lse, dout, gown, gqm, gkm, [gp] + list(rest[11:]), dv, delta_ref
    )


def gp_shapes(length):
    return [(length // h * LEAF, LEAF) for h in halves(length)[1:]]


def run_merge_backward(proj, own, qm, km, p, flat, lab_col, lab_row, attended, lse, dout, scale):
    length = proj.shape[0]
    if length > MERGE_LIMIT:
        levels = [(qm, km, p)] + level_groups(length, flat)
        return long_backward(length, scale, own, proj[:, 2 * LEAF : 3 * LEAF], levels, lab_row, attended, lse, dout)
    operands = [own, proj, qm, km, p, *flat, lab_col, lab_row, attended, lse, dout]
    specs = [plain_spec(x.shape) for x in operands]
    specs[1] = value_spec(length)
    return pl.pallas_call(
        functools.partial(merge_backward_kernel, length, scale),
        grid=(1,),
        in_specs=specs,
        out_specs=[plain_spec((length, LEAF))] * 5,
        out_shape=[matrix(length)] * 5,
        scratch_shapes=[pltpu.VMEM((length, 1), jnp.float32)] + [pltpu.VMEM(shape, jnp.float32) for shape in gp_shapes(length)],
        compiler_params=settings(),
        cost_estimate=cost(1, 1),
        name="merge_backward",
    )(*operands)


EXTRA = 16


def normalize(values):
    return values * lax.rsqrt(jnp.mean(values * values, axis=-1, keepdims=True) + epsilon)


def norm_back(cotangent, normed, values):
    scaled = lax.rsqrt(jnp.mean(values * values, axis=-1, keepdims=True) + epsilon)
    return scaled * (cotangent - normed * jnp.mean(cotangent * normed, axis=-1, keepdims=True))


def dot(a, b, dims=NN):
    return lax.dot_general(a, b, (dims, ((), ())), preferred_element_type=jnp.float32)


def after(value, *others):
    return lax.optimization_barrier((value, *others))[0]


def swap(value, axis):
    return lax.ppermute(value, axis, [(0, 1), (1, 0)])


def by_index(own, other, axis, at):
    first = lax.axis_index(axis) == 0
    return jnp.stack([jnp.where(first, own, other), jnp.where(first, other, own)], axis=at)


def pick(value, at, index):
    return lax.dynamic_index_in_dim(value, index, at, False)


def gather_at(value, at, axis):
    return by_index(value, swap(value, axis), axis, at)


def gathered(value, axes):
    for at, axis in enumerate(axes):
        value = gather_at(value, at, axis)
    return value


def exchange_at(value, at, axis):
    me = lax.axis_index(axis)
    return by_index(pick(value, at, me), swap(pick(value, at, 1 - me), axis), axis, at)


def exchanged(value, axes):
    for at, axis in enumerate(axes):
        value = exchange_at(value, at, axis)
    return value


def scattered(value, axes):
    for at, axis in reversed(list(enumerate(axes))):
        me = lax.axis_index(axis)
        total = pick(value, at, me).astype(jnp.float32) + swap(pick(value, at, 1 - me), axis).astype(jnp.float32)
        value = total if at == 0 else total.astype(value.dtype)
    return value


def scatter_at(value, at, axis):
    me = lax.axis_index(axis)
    came = swap(pick(value, at, 1 - me), axis).astype(jnp.float32)
    return (pick(value, at, me).astype(jnp.float32) + came).astype(value.dtype)


def copies(value, axes):
    return lax.all_to_all(jnp.broadcast_to(value, (lax.axis_size(axes), *value.shape)), axes, 0, 0, tiled=True)


def sums(value, axes):
    value = value.reshape(lax.axis_size(axes), -1, value.shape[-1])
    return jnp.sum(lax.all_to_all(value, axes, 0, 0, tiled=True).astype(jnp.float32), axis=0)


def padded(value, axis, size):
    widths = [(0, 0)] * value.ndim
    widths[axis] = (0, size - value.shape[axis])
    return jnp.pad(value, widths)


def fence(*values):
    return lax.optimization_barrier(values)


def mlp_kernel(units, act_ref, grad_ref, weight_ref, rows_out, hidden_out, part_out):
    both = raw_dot(act_ref[...], weight_ref[:, : 2 * units], NN)
    hidden_grad = raw_dot(grad_ref[...], weight_ref[:, 2 * units :], NN)
    gate, up = both[:, :units], both[:, units:]
    sigmoid_gate = jax.nn.sigmoid(gate)
    silu_gate = gate * sigmoid_gate
    hidden_out[...] = (silu_gate * up).astype(jnp.bfloat16)
    rows_out[:, :units] = (hidden_grad * up * sigmoid_gate * (1.0 + gate * (1.0 - sigmoid_gate))).astype(jnp.bfloat16)
    rows_out[:, units:] = (hidden_grad * silu_gate).astype(jnp.bfloat16)
    part_out[...] = raw_dot(rows_out[...], weight_ref[:, : 2 * units], NT).astype(jnp.bfloat16)


def mlp_of(act, grad, weight):
    tokens, width = act.shape
    units = weight.shape[1] // 3
    outs = [matrix(tokens, 2 * units, jnp.bfloat16), matrix(tokens, units, jnp.bfloat16), matrix(tokens, width, jnp.bfloat16)]
    return pl.pallas_call(
        functools.partial(mlp_kernel, units),
        in_specs=[whole_spec()] * 3,
        out_specs=[whole_spec()] * 3,
        out_shape=outs,
        compiler_params=settings(),
        cost_estimate=cost(1, 1),
        name="mlp",
    )(act, grad, weight)


def mlp_grads_kernel(act_ref, grad_ref, rows_ref, hidden_ref, out):
    wide = rows_ref.shape[1]
    out[:, :wide] = raw_dot(act_ref[...], rows_ref[...], TN).astype(jnp.bfloat16)
    out[:, wide:] = raw_dot(grad_ref[...], hidden_ref[...], TN).astype(jnp.bfloat16)


def mlp_grads_of(act, grad, rows, hidden):
    tokens, width = act.shape
    units = hidden.shape[1]
    step = 2 * LEAF
    column = pl.BlockSpec((tokens, step), lambda i: (0, i))
    return pl.pallas_call(
        mlp_grads_kernel,
        grid=(width // step,),
        in_specs=[column, column, plain_spec(rows.shape), plain_spec(hidden.shape)],
        out_specs=pl.BlockSpec((step, 3 * units), lambda i: (i, 0)),
        out_shape=matrix(width, 3 * units, jnp.bfloat16),
        compiler_params=settings(),
        cost_estimate=cost(1, 1),
        name="mlp_grads",
    )(act, grad, rows, hidden)


GRAD_ROWS = 3 * LEAF


def pair_grads_kernel(rows, in_ref, grad_ref, weight_ref, gain_ref, out, gain_out):
    result = raw_dot(in_ref[...], grad_ref[...], TN)
    beta = result[:, 4 * LEAF :].T[0:1, :]
    low = result[:, : 4 * LEAF].astype(jnp.bfloat16)
    bias = jnp.sum(grad_ref[:, 4 * LEAF :].astype(jnp.float32), axis=0, keepdims=True)
    wide = lambda x: jnp.concatenate([x, jnp.zeros((1, 4 * LEAF - x.shape[1]), jnp.float32)], axis=1)
    small = jnp.concatenate([wide(beta), wide(bias), jnp.zeros((EXTRA - 2, 4 * LEAF), jnp.float32)], axis=0).astype(jnp.bfloat16)
    for i in range(GRAD_ROWS // rows):
        out[i, :rows, :] = low[i * rows : (i + 1) * rows, :]
        out[i, rows:, :] = small
    products = jnp.sum(result * weight_ref[...].astype(jnp.float32), axis=1, keepdims=True)
    gain_out[...] = jnp.broadcast_to(products, (GRAD_ROWS, LEAF)).T[0:1, :] / gain_ref[...]


def pair_grads_of(attn_in, proj_grad, weight, gain, rows):
    length, width = attn_in.shape
    owners = GRAD_ROWS // rows
    row = pl.BlockSpec((1, GRAD_ROWS), lambda i: (0, i))
    return pl.pallas_call(
        functools.partial(pair_grads_kernel, rows),
        grid=(width // GRAD_ROWS,),
        in_specs=[
            pl.BlockSpec((length, GRAD_ROWS), lambda i: (0, i)),
            plain_spec(proj_grad.shape),
            pl.BlockSpec((GRAD_ROWS, weight.shape[1]), lambda i: (i, 0)),
            row,
        ],
        out_specs=[pl.BlockSpec((owners, rows + EXTRA, 4 * LEAF), lambda i: (i, 0, 0)), row],
        out_shape=[
            jax.ShapeDtypeStruct((width // rows, rows + EXTRA, 4 * LEAF), jnp.bfloat16),
            jax.ShapeDtypeStruct((1, width), jnp.float32),
        ],
        compiler_params=settings(),
        cost_estimate=cost(12 * 10**9, 36 * 10**6),
        name="pair_grads",
    )(attn_in, proj_grad, weight, gain.reshape(1, width))


def local(
    steps, tokens, w_query, w_key, w_value, w_house, w_beta, beta_bias, w_out, w_gate, w_up, w_down, gain_attn, gain_mlp, segment_ids, out_grad
):
    outer_axes, inner_axes = steps[:-2], steps[-2:]
    group = ("head", *inner_axes)
    low = jnp.bfloat16
    batches, positions, width = tokens.shape
    half = lax.axis_index("head")
    rank = lax.axis_index(steps)
    count = lax.axis_size(steps)
    inner = lax.axis_size(inner_axes)
    rows, half_heads = w_beta.shape
    assert batches == lax.axis_size("head") == 2 and 2 * half_heads <= count
    length = count * positions
    units = w_gate.shape[1] // inner
    depth = inner * rows
    scale = LEAF ** (-0.5)
    by_half = lambda own, other, at=0: by_index(own, other, "head", at)

    def gathered_outer(value):
        return lax.all_gather(value, outer_axes, axis=0, tiled=True)

    def to_owner(value):
        return exchanged(value.reshape(2, 2, rows, -1), inner_axes).reshape(inner, rows, -1)

    def outer_sums(value):
        return lax.psum_scatter(value, outer_axes, scatter_dimension=0, tiled=True)

    micro = lax.axis_index(steps[0])
    slots = count // 2
    four = (w_query, w_key, w_value, w_house)
    packed = jnp.stack(
        [jnp.concatenate([w[:, i * LEAF : (i + 1) * LEAF] for w in four], axis=1) for i in range(half_heads)]
    )
    beta_row = padded(w_beta.T[:, None, :], 2, 4 * LEAF)
    label_row = jnp.broadcast_to(padded(segment_ids.astype(low).reshape(1, 1, -1), 2, 4 * LEAF), (half_heads, 1, 4 * LEAF))
    packed = padded(padded(jnp.concatenate([packed, beta_row, label_row], axis=1), 1, rows + EXTRA), 0, slots)
    packed = jnp.broadcast_to(packed[None], (2, *packed.shape)).reshape(count, rows + EXTRA, 4 * LEAF)
    both_inputs = tokens.astype(jnp.float32)
    attn_in = exchanged((normalize(both_inputs) * gain_attn).astype(low), steps[:1])
    attn_in = lax.all_gather(attn_in, steps[1:], axis=1, tiled=True).reshape(length, width)
    blocks = [slice(i * units, (i + 1) * units) for i in range(inner)]
    mlp_own = jnp.stack([jnp.concatenate([w_gate[:, i], w_up[:, i], w_down[i].T], axis=1) for i in blocks])
    mlp_own = exchanged(mlp_own.reshape(2, 2, rows, 3 * units), inner_axes[:1])
    out_own = gathered(w_out.T, outer_axes)

    packed, mlp_own, out_own = fence(packed, mlp_own, out_own)

    packed = lax.all_to_all(packed, steps, 0, 0, tiled=True)
    mlp_own = exchange_at(mlp_own, 1, inner_axes[1]).reshape(depth, 3 * units)
    weight = packed[:, :rows].reshape(width, 4 * LEAF)
    beta_column = padded(packed[:, rows, :rows].reshape(width, 1), 1, LEAF)
    weight = jnp.concatenate([weight, beta_column], axis=1)
    label_all = pick(packed[:, rows + 1, : 2 * positions].reshape(count, 2, positions), 1, micro)
    label_all = label_all.reshape(1, length).astype(jnp.float32)
    label_column = jnp.broadcast_to(label_all.reshape(length, 1), (length, LEAF))
    weight, label_all, label_column, attn_in, mlp_own, out_own = fence(
        weight, label_all, label_column, attn_in, mlp_own, out_own
    )

    bias_row = padded(lax.dynamic_slice(padded(beta_bias, 0, slots), (rank % slots,), (1,)), 0, LEAF)
    bias_row = jnp.concatenate([jnp.zeros(4 * LEAF, jnp.float32), bias_row])
    proj = dot(attn_in, weight) + bias_row
    mlp_weight = gathered_outer(mlp_own)
    proj, out_own = fence(proj, out_own)

    out_own = gather_at(out_own, len(outer_axes), inner_axes[0])
    *saved, own_logits, query_moved, key_moved, product = leaf_forward(proj)
    own_logits, out_own = fence(own_logits, out_own)

    out_own = gather_at(out_own, len(outer_axes) + 1, inner_axes[1])
    attended, attended_low, log_total, *levels = run_merge_forward(
        proj, own_logits, query_moved, key_moved, product, label_column, label_all, scale
    )
    attended_low, out_own = fence(attended_low, out_own)
    out_own = out_own.reshape(width, half_heads * LEAF)

    grad_group = gather_at(gather_at(after(out_grad, attended_low), 1, inner_axes[0]), 2, inner_axes[1]).reshape(-1, width)
    heads_here = lax.all_to_all(attended_low.reshape(count, positions, LEAF), steps, 0, 0, tiled=True)
    heads_here = heads_here.reshape(2, slots, positions, LEAF)[:, :half_heads].transpose(0, 2, 1, 3)
    heads_here = heads_here.reshape(2 * positions, half_heads * LEAF)
    branch = dot(heads_here, out_own, NT).reshape(2, positions, width)
    branch = pick(branch, 0, half) + swap(pick(branch, 0, 1 - half).astype(low), "head").astype(jnp.float32)
    inputs = pick(tokens, 0, half).astype(jnp.float32)
    middle = inputs + branch
    normed_two = normalize(middle)
    mlp_in = (normed_two * gain_mlp).astype(low)
    mlp_group = copies(mlp_in, group).reshape(-1, width)
    columns = heads_here.reshape(2 * positions, inner, -1).transpose(1, 0, 2)
    columns = columns.reshape(2, 2, 2 * positions, -1)
    mlp_group, mlp_weight, grad_group = fence(mlp_group, mlp_weight, grad_group)

    rows_grad, hidden, mlp_in_part = mlp_of(mlp_group, grad_group, mlp_weight)
    mlp_in_grad = sums(mlp_in_part, group)
    mlp_grads = mlp_grads_of(mlp_group, grad_group, rows_grad, hidden)
    mlp_sums = outer_sums(mlp_grads)
    mlp_part = dot(hidden, mlp_weight[:, 2 * units :], NT).astype(low)
    columns = exchange_at(after(columns, mlp_grads), 0, inner_axes[0])
    mlp_in_grad, mlp_part, columns, mlp_grads = fence(mlp_in_grad, mlp_part, columns, mlp_grads)

    mlp_gain_part = jnp.sum(mlp_in_grad * normed_two, axis=0)
    own_grad = pick(out_grad, 0, half).astype(jnp.float32)
    middle_grad = own_grad + norm_back(mlp_in_grad * gain_mlp, normed_two, middle)
    branch_low = middle_grad.astype(low)
    branch_low = by_half(branch_low, swap(branch_low, "head"))
    attended_grad = dot(branch_low.reshape(2 * positions, width), out_own).astype(low)
    attended_grad = attended_grad.reshape(2, positions, half_heads, LEAF).transpose(0, 2, 1, 3)
    attended_grad = padded(attended_grad, 1, slots).reshape(count, positions, LEAF)
    attended_grad = lax.all_to_all(attended_grad, steps, 0, 0, tiled=True).reshape(length, LEAF).astype(jnp.float32)
    attended_grad, branch_low, mlp_part = fence(attended_grad, branch_low, mlp_part)

    mlp_part = scatter_at(mlp_part.reshape(2, 2, 2, positions, width), 0, "head")
    merged = run_merge_backward(
        proj, own_logits, query_moved, key_moved, product, levels, label_column, label_all, attended, log_total, attended_grad, scale
    )
    branch_group = gather_at(branch_low, 1, inner_axes[0])
    mlp_part, mlp_sums, branch_group, *merged = fence(mlp_part, mlp_sums, branch_group, *merged)

    mlp_part = scatter_at(mlp_part, 1, inner_axes[1])
    mlp_sums = exchange_at(mlp_sums.reshape(2, 2, rows, 3 * units), 0, inner_axes[0])
    middle_both = by_half(middle_grad, swap(middle_grad, "head"))
    proj_grad = leaf_backward(proj, saved, merged)
    branch_group = gather_at(branch_group, 2, inner_axes[1]).reshape(-1, width)
    proj_grad, mlp_part, middle_both, mlp_sums, branch_group = fence(proj_grad, mlp_part, middle_both, mlp_sums, branch_group)

    attn_in_part = dot(proj_grad, weight, NT).astype(low).reshape(*(2,) * len(steps), positions, width)
    packed_grad, attn_gain_part = pair_grads_of(attn_in, proj_grad, weight, gain_attn, rows)
    attn_in_part = scatter_at(attn_in_part, len(steps) - 1, steps[-1])
    mlp_grads = exchange_at(mlp_sums, 1, inner_axes[1]).reshape(inner, rows, 3 * units)
    mlp_part = scatter_at(mlp_part, 0, inner_axes[0])
    columns = exchange_at(columns, 1, inner_axes[1]).reshape(inner, 2, positions, -1)
    packed_grad, attn_gain_part, attn_in_part, mlp_grads, mlp_part, columns = fence(
        packed_grad, attn_gain_part, attn_in_part, mlp_grads, mlp_part, columns
    )

    packed_grad = lax.all_to_all(packed_grad, steps, 0, 0, tiled=True)
    attn_in_part = scatter_at(attn_in_part, 0, "head")
    for at in range(len(steps) - 2, 0, -1):
        attn_in_part = scatter_at(attn_in_part, at - 1, steps[at])
    gains = jnp.stack([attn_gain_part[0], mlp_gain_part])
    for axis in (*inner_axes, "head"):
        gains = gains + swap(gains, axis)
    columns = columns.swapaxes(0, 1).reshape(-1, columns.shape[-1])
    out_weight_grad = dot(branch_group, columns, TN).astype(low).reshape(count, rows, -1)
    mlp_grads = mlp_grads.astype(jnp.float32)
    gate_grad, up_grad = (
        mlp_grads[:, :, i * units : (i + 1) * units].transpose(1, 0, 2).reshape(rows, inner * units) for i in range(2)
    )
    down_grad = mlp_grads[:, :, 2 * units :].transpose(0, 2, 1).reshape(inner * units, rows)
    packed_grad, attn_in_part, mlp_part, gains, out_weight_grad, gate_grad, up_grad, down_grad = fence(
        packed_grad, attn_in_part, mlp_part, gains, out_weight_grad, gate_grad, up_grad, down_grad
    )

    plane = (steps[0], "head")
    same = lax.ppermute(attn_in_part, plane, [(0, 0), (1, 2), (2, 1), (3, 3)])
    opposite = lax.ppermute(attn_in_part, plane, [(0, 1), (1, 3), (2, 0), (3, 2)])
    attn_in_grad = by_half(same, opposite).astype(jnp.float32)

    block_out = (middle + mlp_part).astype(low)
    block_out = by_half(block_out, swap(block_out, "head"))
    out_weight_grad = lax.all_to_all(out_weight_grad, steps, 0, 0, tiled=True).astype(jnp.float32)
    out_weight_grad = jnp.sum(out_weight_grad.reshape(-1, inner, rows, out_weight_grad.shape[-1]), axis=0)
    out_weight_grad = out_weight_grad.transpose(0, 2, 1).reshape(-1, rows)

    for axis in outer_axes:
        gains = gains + swap(gains, axis)
    small = after(packed_grad[:, rows : rows + 2], gains)
    small = jnp.sum(small.reshape(2, slots, 2, -1)[:, :half_heads].astype(jnp.float32), axis=0)
    turn = rank % (GRAD_ROWS // rows) * rows
    beta_grad = lax.dynamic_slice(small[:, 0], (0, turn), (half_heads, rows)).T
    bias_grad = small[:, 1, 0]
    total = packed_grad[:, :rows].reshape(2, slots, rows, -1)[:, :half_heads].astype(jnp.float32)
    total = total[0] + total[1]
    grads = [total[..., i * LEAF : (i + 1) * LEAF].transpose(1, 0, 2).reshape(rows, half_heads * LEAF) for i in range(4)]

    attn_in_grad = after(attn_in_grad, *grads)
    tokens_grad = middle_both + norm_back(attn_in_grad * gain_attn, normalize(both_inputs), both_inputs)
    return (
        block_out, tokens_grad, *grads, beta_grad, bias_grad, out_weight_grad, gate_grad, up_grad, down_grad, gains[0], gains[1]
    )


def solution(mesh):
    depth = mesh.shape["seq"].bit_length() - 1
    assert mesh.shape["seq"] == 2**depth and mesh.shape["head"] == 2
    steps = tuple(f"s{i}" for i in range(depth))
    fine = Mesh(mesh.devices.reshape(*(2,) * depth, 2), (*steps, "head"))
    split_rows, split_columns, by_position = P(steps, "head"), P("head", steps), P(None, steps, None)
    placed = (
        (by_position,) + (split_rows,) * 5 + (P("head"), split_columns, split_rows, split_rows, split_columns)
        + (P(), P(), P(None, steps), by_position)
    )
    returned = (
        (by_position, by_position) + (split_rows,) * 5 + (P("head"), split_columns, split_rows, split_rows, split_columns, P(), P())
    )
    return jax.shard_map(functools.partial(local, steps), mesh=fine, in_specs=placed, out_specs=returned, check_vma=False)
```

```python
import functools

import jax
import jax.numpy as jnp
from jax import lax
from jax.experimental import pallas as pl
from jax.experimental.pallas import tpu as pltpu
from jax.sharding import Mesh
from jax.sharding import PartitionSpec as P

epsilon = 1e-06
masked_score = -1e30
MERGE_LIMIT = 2048
LEAF = 128
NN, NT, TN = ((1,), (0,)), ((1,), (1,)), ((0,), (0,))


def split(a):
    if isinstance(a, tuple):
        return a
    if a.dtype == jnp.bfloat16:
        return (a, None)
    high = a.astype(jnp.bfloat16)
    return (high, (a - high.astype(jnp.float32)).astype(jnp.bfloat16))


def raw_dot(a, b, dims):
    return lax.dot_general(a, b, (dims, ((), ())), preferred_element_type=jnp.float32)


def dot_parts(a, b, dims):
    (ah, al), (bh, bl) = split(a), split(b)
    total = raw_dot(ah, bh, dims)
    if bl is not None:
        total = total + raw_dot(ah, bl, dims)
    if al is not None:
        total = total + raw_dot(al, bh, dims)
    return total


def grid_of(shape, axis):
    return lax.broadcasted_iota(jnp.int32, shape, axis)


def leaf_masks():
    row, col = grid_of((LEAF, LEAF), 0), grid_of((LEAF, LEAF), 1)
    return row, col


def leaf_forward_kernel(leaves, q_ref, k_ref, h_ref, g_ref, x_out, a_out, c_out, u_out, w_out, tm_out, dots_out, own_out, qm_out, km_out, p_out):
    mm = dot_parts
    row, col = leaf_masks()
    eye = (row == col).astype(jnp.float32)
    span = range(leaves)
    at = [pl.ds(g * LEAF, LEAF) for g in span]
    q = [split(q_ref[i, :]) for i in at]
    k = [split(k_ref[i, :]) for i in at]
    mirror, strength = [], []
    for i in at:
        h = h_ref[i, :]
        mirror.append(split(h * lax.rsqrt(jnp.sum(h * h, axis=-1, keepdims=True) + epsilon)))
        strength.append(2.0 * jax.nn.sigmoid(jnp.broadcast_to(g_ref[i, 0:1], (LEAF, LEAF))))
    dots = [mm(m, m, NT) for m in mirror]
    system = [jnp.where(row > col, d, 0.0) * s for d, s in zip(dots, strength)]
    inverse = [eye - jnp.where((row // 2 == col // 2), n, 0.0) for n in system]
    width = 2
    while width < LEAF:
        picked = (row // (2 * width) == col // (2 * width)) & (row // width != col // width)
        parts = [split(x) for x in inverse]
        off = [split(jnp.where(picked, n, 0.0)) for n in system]
        turned = [mm(x, n, NN) for x, n in zip(parts, off)]
        inverse = [x - mm(t, p, NN) for x, t, p in zip(inverse, turned, parts)]
        width *= 2
    triang = [split(x * s.T) for x, s in zip(inverse, strength)]
    a_part = [split(jnp.where(row >= col, mm(x, m, NT), 0.0)) for x, m in zip(q, mirror)]
    c_part = [split(jnp.where(row < col, mm(x, m, NT), 0.0)) for x, m in zip(k, mirror)]
    own = [mm(x, y, NT) for x, y in zip(q, k)]
    u_part = [split(mm(x, t, NN)) for x, t in zip(a_part, triang)]
    w_part = [split(mm(x, t, NT)) for x, t in zip(c_part, triang)]
    tm_part = [split(mm(t, m, NN)) for t, m in zip(triang, mirror)]
    for g, i in enumerate(at):
        x_out[i, :] = inverse[g]
        dots_out[i, :] = dots[g]
        for ref, value in ((a_out, a_part), (c_out, c_part), (u_out, u_part), (w_out, w_part), (tm_out, tm_part)):
            high, low = value[g]
            ref[i, :] = high.astype(jnp.float32) + low.astype(jnp.float32)
        own_out[i, :] = own[g] - mm(u_part[g], c_part[g], NT)
        qm_out[i, :] = q_ref[i, :] - mm(u_part[g], mirror[g], NN)
        km_out[i, :] = k_ref[i, :] - mm(w_part[g], mirror[g], NN)
        p_out[i, :] = eye - mm(mirror[g], tm_part[g], TN)


def leaf_backward_kernel(leaves, q_ref, k_ref, h_ref, g_ref, x_ref, a_ref, c_ref, u_ref, w_ref, tm_ref, dots_ref, gown_ref, gqm_ref, gkm_ref, gp_ref, dv_ref, out):
    mm = dot_parts
    row, col = leaf_masks()
    ones = jnp.ones((LEAF, LEAF), jnp.bfloat16)
    at = [pl.ds(g * LEAF, LEAF) for g in range(leaves)]
    q = [split(q_ref[i, :]) for i in at]
    k = [split(k_ref[i, :]) for i in at]
    h = [h_ref[i, :] for i in at]
    scaling = [lax.rsqrt(jnp.sum(x * x, axis=-1, keepdims=True) + epsilon) for x in h]
    mirror_full = [x * r for x, r in zip(h, scaling)]
    mirror = [split(x) for x in mirror_full]
    strength = [2.0 * jax.nn.sigmoid(jnp.broadcast_to(g_ref[i, 0:1], (LEAF, LEAF))) for i in at]
    inverse_full = [x_ref[i, :] for i in at]
    inverse = [split(x) for x in inverse_full]
    strength_row = [s.T for s in strength]
    triang = [split(x * s) for x, s in zip(inverse_full, strength_row)]
    a_part = [split(a_ref[i, :]) for i in at]
    c_part = [split(c_ref[i, :]) for i in at]
    u_part = [split(u_ref[i, :]) for i in at]
    w_part = [split(w_ref[i, :]) for i in at]
    tm_part = [split(tm_ref[i, :]) for i in at]
    gown = [split(gown_ref[i, :]) for i in at]
    gqm = [split(gqm_ref[i, :]) for i in at]
    gkm = [split(gkm_ref[i, :]) for i in at]
    gp = [split(gp_ref[i, :]) for i in at]
    span = range(leaves)
    gu = [split(-mm(gqm[g], mirror[g], NT) - mm(gown[g], c_part[g], NN)) for g in span]
    gw = [split(-mm(gkm[g], mirror[g], NT)) for g in span]
    mgp = [split(mm(mirror[g], gp[g], NN)) for g in span]
    ga = [split(jnp.where(row >= col, mm(gu[g], triang[g], NT), 0.0)) for g in span]
    gc = [split(jnp.where(row < col, mm(gw[g], triang[g], NN) - mm(gown[g], u_part[g], TN), 0.0)) for g in span]
    gt = [mm(a_part[g], gu[g], TN) + mm(gw[g], c_part[g], TN) - mm(mgp[g], mirror[g], NT) for g in span]
    gx = [split(gt[g] * strength_row[g]) for g in span]
    xgx = [split(mm(inverse[g], gx[g], TN)) for g in span]
    gn = [jnp.where(row > col, -mm(xgx[g], inverse[g], NT), 0.0) for g in span]
    gdots = [split(strength[g] * gn[g]) for g in span]
    for g, i in enumerate(at):
        gm = (
            -mm(u_part[g], gqm[g], TN)
            - mm(w_part[g], gkm[g], TN)
            + mm(ga[g], q[g], TN)
            + mm(gc[g], k[g], TN)
            + mm(gdots[g], mirror[g], NN)
            + mm(gdots[g], mirror[g], TN)
            - mm(tm_part[g], gp[g], NT)
            - mm(triang[g], mgp[g], TN)
        )
        gq = gqm_ref[i, :] + mm(gown[g], k[g], NN) + mm(ga[g], mirror[g], NN)
        gk = gkm_ref[i, :] + mm(gown[g], q[g], TN) + mm(gc[g], mirror[g], NN)
        gh = scaling[g] * (gm - mirror_full[g] * jnp.sum(gm * mirror_full[g], axis=-1, keepdims=True))
        gs = mm(gn[g] * dots_ref[i, :], ones, NN) + mm(gt[g] * inverse_full[g], ones, TN)
        gl = gs * strength[g] * (1.0 - 0.5 * strength[g])
        out[i, 0:128] = gq.astype(jnp.bfloat16)
        out[i, 128:256] = gk.astype(jnp.bfloat16)
        out[i, 256:384] = dv_ref[i, :].astype(jnp.bfloat16)
        out[i, 384:512] = gh.astype(jnp.bfloat16)
        out[i, 512:640] = jnp.where(col == 0, gl, 0.0).astype(jnp.bfloat16)


def halves(length):
    found, h = [], LEAF
    while h < length:
        found.append(h)
        h *= 2
    return found


def merge_forward(length, scale, own, v, qm, km, p, lab_col, lab_row, attended, attended_low, lse, levels, m_ref, l_ref, o_ref):
    mm = dot_parts
    row, col = leaf_masks()
    for start in range(0, length, LEAF):
        i = slice(start, start + LEAF)
        allowed = (row >= col) & (lab_col[i, 0:1] == lab_row[:, i])
        scores = jnp.where(allowed, own[i, :] * scale, masked_score)
        top = jnp.max(scores, axis=-1, keepdims=True)
        weights = jnp.exp(scores - top)
        m_ref[i, :] = top
        l_ref[i, :] = jnp.sum(weights, axis=-1, keepdims=True)
        o_ref[i, :] = mm(weights, v[i, :], NN)
    sizes = halves(length)
    for step, h in enumerate(sizes):
        last = step + 1 == len(sizes)
        if not last:
            qm_next, km_next, p_next = levels[step]
        for start in range(0, length, 2 * h):
            a, b = slice(start, start + h), slice(start + h, start + 2 * h)
            pa = slice(start // h * LEAF, start // h * LEAF + LEAF)
            pb = slice(start // h * LEAF + LEAF, start // h * LEAF + 2 * LEAF)
            qm_b, km_a = split(qm[b, :]), split(km[a, :])
            scores = mm(qm_b, km_a, NT) * scale
            scores = jnp.where(lab_col[b, 0:1] == lab_row[:, a], scores, masked_score)
            old = m_ref[b, :]
            top = jnp.maximum(old, jnp.max(scores, axis=-1, keepdims=True))
            factor = jnp.exp(old - top)
            weights = jnp.exp(scores - top)
            m_ref[b, :] = top
            l_ref[b, :] = l_ref[b, :] * factor + jnp.sum(weights, axis=-1, keepdims=True)
            o_ref[b, :] = o_ref[b, :] * factor + mm(weights, v[a, :], NN)
            if not last:
                p_a, p_b = split(p[pa, :]), split(p[pb, :])
                qm_next[a, :] = qm[a, :]
                qm_next[b, :] = mm(qm_b, p_a, NN)
                km_next[b, :] = km[b, :]
                km_next[a, :] = mm(km_a, p_b, NT)
                if p_next is not None:
                    into = start // (2 * h) * LEAF
                    p_next[slice(into, into + LEAF), :] = mm(p_b, p_a, NN)
        if not last:
            qm, km, p = qm_next, km_next, p_next
    total = l_ref[...]
    result = o_ref[...] / total
    attended[...] = result
    attended_low[...] = result.astype(jnp.bfloat16)
    lse[...] = jnp.broadcast_to(m_ref[...] + jnp.log(total), (length, LEAF))


def merge_backward(length, scale, own, v, levels, lab_col, lab_row, attended, lse, dout, gown, gqm, gkm, gp, dv, delta_ref):
    mm = dot_parts
    row, col = leaf_masks()
    delta_ref[...] = jnp.sum(dout[...] * attended[...], axis=-1, keepdims=True)
    for start in range(0, length, LEAF):
        i = slice(start, start + LEAF)
        allowed = (row >= col) & (lab_col[i, 0:1] == lab_row[:, i])
        probs = jnp.where(allowed, jnp.exp(own[i, :] * scale - lse[i, 0:1]), 0.0)
        grad = split(dout[i, :])
        dv[i, :] = mm(probs, grad, TN)
        gown[i, :] = probs * (mm(grad, v[i, :], NT) - delta_ref[i, :]) * scale
    sizes = halves(length)
    for step in reversed(range(len(sizes))):
        h = sizes[step]
        last = step + 1 == len(sizes)
        qm, km, p = levels[step]
        for start in range(0, length, 2 * h):
            a, b = slice(start, start + h), slice(start + h, start + 2 * h)
            pa = slice(start // h * LEAF, start // h * LEAF + LEAF)
            pb = slice(start // h * LEAF + LEAF, start // h * LEAF + 2 * LEAF)
            qm_b, km_a, grad = split(qm[b, :]), split(km[a, :]), split(dout[b, :])
            scores = mm(qm_b, km_a, NT) * scale
            allowed = lab_col[b, 0:1] == lab_row[:, a]
            probs = jnp.where(allowed, jnp.exp(scores - lse[b, 0:1]), 0.0)
            dv[a, :] = dv[a, :] + mm(probs, grad, TN)
            ds = split(probs * (mm(grad, v[a, :], NT) - delta_ref[b, :]) * scale)
            gq_part = mm(ds, km_a, NN)
            gk_part = mm(ds, qm_b, TN)
            if last:
                gqm[a, :] = jnp.zeros((h, LEAF), jnp.float32)
                gkm[b, :] = jnp.zeros((h, LEAF), jnp.float32)
                gqm[b, :] = gq_part
                gkm[a, :] = gk_part
            else:
                p_a, p_b = split(p[pa, :]), split(p[pb, :])
                gq_b, gk_a = split(gqm[b, :]), split(gkm[a, :])
                gp_a, gp_b = mm(qm_b, gq_b, TN), mm(gk_a, km_a, TN)
                if step + 2 < len(sizes):
                    into = start // (2 * h) * LEAF
                    g_up = split(gp[step + 1][slice(into, into + LEAF), :])
                    gp_a, gp_b = gp_a + mm(p_b, g_up, TN), gp_b + mm(g_up, p_a, NT)
                gp[step][pa, :] = gp_a
                gp[step][pb, :] = gp_b
                gqm[b, :] = mm(gq_b, p_a, NT) + gq_part
                gkm[a, :] = mm(gk_a, p_b, NN) + gk_part


def whole_dot(spec, *operands):
    return jnp.einsum(spec, *operands, precision=lax.Precision.HIGHEST)


def pairs(value, size):
    both = value.reshape(-1, 2, size, value.shape[-1])
    return both[:, 0], both[:, 1]


def joined(first, second):
    return jnp.stack([first, second], axis=1).reshape(-1, first.shape[-1])


def long_allowed(label, size, own):
    both = label.reshape(-1, size) if own else label.reshape(-1, 2, size)
    left, right = (both, both) if own else (both[:, 0], both[:, 1])
    same = right[:, :, None] == left[:, None, :]
    return same & jnp.tril(jnp.ones((size, size), jnp.bool_)) if own else same


def long_forward(length, scale, own, v, qm, km, p, label):
    scores = jnp.where(long_allowed(label, LEAF, True), own.reshape(-1, LEAF, LEAF) * scale, masked_score)
    top = jnp.max(scores, axis=-1, keepdims=True)
    weights = jnp.exp(scores - top)
    state = [
        x.reshape(length, -1)
        for x in (top, jnp.sum(weights, axis=-1, keepdims=True), whole_dot("nij,njd->nid", weights, v.reshape(-1, LEAF, LEAF)))
    ]
    levels = []
    for h in halves(length):
        (q_a, q_b), (k_a, k_b), (v_a, _) = pairs(qm, h), pairs(km, h), pairs(v, h)
        scores = whole_dot("nid,njd->nij", q_b, k_a) * scale
        scores = jnp.where(long_allowed(label, h, False), scores, masked_score)
        (m_a, m_b), (l_a, l_b), (o_a, o_b) = (pairs(x, h) for x in state)
        top = jnp.maximum(m_b, jnp.max(scores, axis=-1, keepdims=True))
        factor = jnp.exp(m_b - top)
        weights = jnp.exp(scores - top)
        l_b = l_b * factor + jnp.sum(weights, axis=-1, keepdims=True)
        o_b = o_b * factor + whole_dot("nij,njd->nid", weights, v_a)
        state = [joined(m_a, top), joined(l_a, l_b), joined(o_a, o_b)]
        if 2 * h < length:
            p_a, p_b = pairs(p, LEAF)
            qm = joined(q_a, whole_dot("nid,nde->nie", q_b, p_a))
            km = joined(whole_dot("nid,ned->nie", k_a, p_b), k_b)
            p = whole_dot("nde,nef->ndf", p_b, p_a).reshape(-1, LEAF)
            levels += [qm, km] + ([p] if 4 * h < length else [])
    top, total, out = state
    return [out / total, (out / total).astype(jnp.bfloat16), jnp.broadcast_to(top + jnp.log(total), (length, LEAF))] + levels


def long_backward(length, scale, own, v, levels, label, attended, lse, dout):
    lse = lse[:, :1]
    delta = jnp.sum(dout * attended, axis=-1, keepdims=True)
    blocks = lambda x: x.reshape(length // LEAF, LEAF, -1)
    probs = jnp.exp(blocks(own) * scale - blocks(lse))
    probs = jnp.where(long_allowed(label, LEAF, True), probs, 0.0)
    dv = whole_dot("nij,nid->njd", probs, blocks(dout)).reshape(length, LEAF)
    gown = probs * (whole_dot("nid,njd->nij", blocks(dout), blocks(v)) - blocks(delta)) * scale
    gqm = gkm = gp = None
    for h, (qm, km, p) in reversed(list(zip(halves(length), levels))):
        (_, q_b), (k_a, _), (v_a, _), (_, o_b) = pairs(qm, h), pairs(km, h), pairs(v, h), pairs(dout, h)
        scores = whole_dot("nid,njd->nij", q_b, k_a) * scale - pairs(lse, h)[1]
        probs = jnp.where(long_allowed(label, h, False), jnp.exp(scores), 0.0)
        dv_a, dv_b = pairs(dv, h)
        dv = joined(dv_a + whole_dot("nij,nid->njd", probs, o_b), dv_b)
        ds = probs * (whole_dot("nid,njd->nij", o_b, v_a) - pairs(delta, h)[1]) * scale
        gq_part, gk_part = whole_dot("nij,njd->nid", ds, k_a), whole_dot("nij,nid->njd", ds, q_b)
        if gqm is None:
            gqm, gkm = joined(jnp.zeros_like(gq_part), gq_part), joined(gk_part, jnp.zeros_like(gk_part))
            continue
        (gq_a, gq_b), (gk_a, gk_b), (p_a, p_b) = pairs(gqm, h), pairs(gkm, h), pairs(p, LEAF)
        gp_a, gp_b = whole_dot("nid,nie->nde", q_b, gq_b), whole_dot("nid,nie->nde", gk_a, k_a)
        if gp is not None:
            above = gp.reshape(-1, LEAF, LEAF)
            gp_a = gp_a + whole_dot("nde,ndf->nef", p_b, above)
            gp_b = gp_b + whole_dot("ndf,nef->nde", above, p_a)
        gp = joined(gp_a, gp_b)
        gqm = joined(gq_a, whole_dot("nid,ned->nie", gq_b, p_a) + gq_part)
        gkm = joined(whole_dot("nid,nde->nie", gk_a, p_b) + gk_part, gk_b)
    return [gown.reshape(length, LEAF), gqm, gkm, gp, dv]


def matrix(rows, columns=LEAF, dtype=jnp.float32):
    return jax.ShapeDtypeStruct((rows, columns), dtype)


def cost(flops, moved):
    return pl.CostEstimate(flops=flops, bytes_accessed=moved, transcendentals=0)


def settings():
    return pltpu.CompilerParams(vmem_limit_bytes=56 * 1024 * 1024)


def leaf_group(length, most):
    leaves = length // LEAF
    return next(g for g in (most, 4, 2, 1) if leaves % g == 0)


def leaf_forward(proj):
    length = proj.shape[0]
    leaves = leaf_group(length, 8)
    rows = leaves * LEAF
    column = lambda j: pl.BlockSpec((rows, LEAF), lambda i, j=j: (i, j))
    return pl.pallas_call(
        functools.partial(leaf_forward_kernel, leaves),
        grid=(length // rows,),
        in_specs=[column(0), column(1), column(3), column(4)],
        out_specs=[column(0)] * 11,
        out_shape=[matrix(length)] * 11,
        compiler_params=settings(),
        cost_estimate=cost(1, 1),
        name="leaf_forward",
    )(proj, proj, proj, proj)


def leaf_backward(proj, saved, grads):
    length = proj.shape[0]
    leaves = leaf_group(length, 4)
    rows = leaves * LEAF
    column = lambda j: pl.BlockSpec((rows, LEAF), lambda i, j=j: (i, j))
    return pl.pallas_call(
        functools.partial(leaf_backward_kernel, leaves),
        grid=(length // rows,),
        in_specs=[column(0), column(1), column(3), column(4)] + [column(0)] * (len(saved) + len(grads)),
        out_specs=pl.BlockSpec((rows, 5 * LEAF), lambda i: (i, 0)),
        out_shape=matrix(length, 5 * LEAF, jnp.bfloat16),
        compiler_params=settings(),
        cost_estimate=cost(1, 1),
        name="leaf_backward",
    )(proj, proj, proj, proj, *saved, *grads)


def level_shapes(length):
    sizes = halves(length)
    shapes = []
    for step in range(1, len(sizes)):
        shapes += [matrix(length), matrix(length)]
        if step + 1 < len(sizes):
            shapes.append(matrix(length // sizes[step] * LEAF))
    return shapes


def level_groups(length, flat):
    sizes, groups, flat = halves(length), [], list(flat)
    for step in range(1, len(sizes)):
        qm, km = flat.pop(0), flat.pop(0)
        groups.append((qm, km, flat.pop(0) if step + 1 < len(sizes) else None))
    return groups


def whole_spec():
    return pl.BlockSpec(memory_space=pltpu.VMEM)


def value_spec(length):
    return pl.BlockSpec((length, LEAF), lambda i: (0, 2))


def plain_spec(shape):
    return pl.BlockSpec(shape, lambda i: (0, 0))


def merge_forward_kernel(length, scale, own, v, qm, km, p, lab_col, lab_row, attended, attended_low, lse, *rest):
    flat, (m_ref, l_ref, o_ref) = rest[:-3], rest[-3:]
    merge_forward(
        length, scale, own, v, qm, km, p, lab_col, lab_row, attended, attended_low, lse, level_groups(length, flat), m_ref, l_ref, o_ref
    )


def run_merge_forward(proj, own, qm, km, p, lab_col, lab_row, scale):
    length = proj.shape[0]
    extra = level_shapes(length)
    if length > MERGE_LIMIT:
        return long_forward(length, scale, own, proj[:, 2 * LEAF : 3 * LEAF], qm, km, p, lab_row)
    outs = [matrix(length), matrix(length, LEAF, jnp.bfloat16), matrix(length)] + extra
    return pl.pallas_call(
        functools.partial(merge_forward_kernel, length, scale),
        grid=(1,),
        in_specs=[plain_spec(own.shape), value_spec(length)] + [plain_spec(x.shape) for x in (qm, km, p, lab_col, lab_row)],
        out_specs=[plain_spec(x.shape) for x in outs],
        out_shape=outs,
        scratch_shapes=[pltpu.VMEM((length, 1), jnp.float32), pltpu.VMEM((length, 1), jnp.float32), pltpu.VMEM((length, LEAF), jnp.float32)],
        compiler_params=settings(),
        cost_estimate=cost(1, 1),
        name="merge_forward",
    )(own, proj, qm, km, p, lab_col, lab_row)


def merge_backward_kernel(length, scale, own, v, qm, km, p, *rest):
    count = len(level_shapes(length))
    flat, rest = rest[:count], rest[count:]
    lab_col, lab_row, attended, lse, dout, gown, gqm, gkm, gp, dv, delta_ref = rest[:11]
    levels = [(qm, km, p)] + level_groups(length, flat)
    merge_backward(
        length, scale, own, v, levels, lab_col, lab_row, attended, lse, dout, gown, gqm, gkm, [gp] + list(rest[11:]), dv, delta_ref
    )


def gp_shapes(length):
    return [(length // h * LEAF, LEAF) for h in halves(length)[1:]]


def run_merge_backward(proj, own, qm, km, p, flat, lab_col, lab_row, attended, lse, dout, scale):
    length = proj.shape[0]
    if length > MERGE_LIMIT:
        levels = [(qm, km, p)] + level_groups(length, flat)
        return long_backward(length, scale, own, proj[:, 2 * LEAF : 3 * LEAF], levels, lab_row, attended, lse, dout)
    operands = [own, proj, qm, km, p, *flat, lab_col, lab_row, attended, lse, dout]
    specs = [plain_spec(x.shape) for x in operands]
    specs[1] = value_spec(length)
    return pl.pallas_call(
        functools.partial(merge_backward_kernel, length, scale),
        grid=(1,),
        in_specs=specs,
        out_specs=[plain_spec((length, LEAF))] * 5,
        out_shape=[matrix(length)] * 5,
        scratch_shapes=[pltpu.VMEM((length, 1), jnp.float32)] + [pltpu.VMEM(shape, jnp.float32) for shape in gp_shapes(length)],
        compiler_params=settings(),
        cost_estimate=cost(1, 1),
        name="merge_backward",
    )(*operands)


EXTRA = 16


def normalize(values):
    return values * lax.rsqrt(jnp.mean(values * values, axis=-1, keepdims=True) + epsilon)


def norm_back(cotangent, normed, values):
    scaled = lax.rsqrt(jnp.mean(values * values, axis=-1, keepdims=True) + epsilon)
    return scaled * (cotangent - normed * jnp.mean(cotangent * normed, axis=-1, keepdims=True))


def dot(a, b, dims=NN):
    return lax.dot_general(a, b, (dims, ((), ())), preferred_element_type=jnp.float32)


def after(value, *others):
    return lax.optimization_barrier((value, *others))[0]


def swap(value, axis):
    return lax.ppermute(value, axis, [(0, 1), (1, 0)])


def by_index(own, other, axis, at):
    first = lax.axis_index(axis) == 0
    return jnp.stack([jnp.where(first, own, other), jnp.where(first, other, own)], axis=at)


def pick(value, at, index):
    return lax.dynamic_index_in_dim(value, index, at, False)


def gather_at(value, at, axis):
    return by_index(value, swap(value, axis), axis, at)


def gathered(value, axes):
    for at, axis in enumerate(axes):
        value = gather_at(value, at, axis)
    return value


def exchange_at(value, at, axis):
    me = lax.axis_index(axis)
    return by_index(pick(value, at, me), swap(pick(value, at, 1 - me), axis), axis, at)


def exchanged(value, axes):
    for at, axis in enumerate(axes):
        value = exchange_at(value, at, axis)
    return value


def scattered(value, axes):
    for at, axis in reversed(list(enumerate(axes))):
        me = lax.axis_index(axis)
        total = pick(value, at, me).astype(jnp.float32) + swap(pick(value, at, 1 - me), axis).astype(jnp.float32)
        value = total if at == 0 else total.astype(value.dtype)
    return value


def scatter_at(value, at, axis):
    me = lax.axis_index(axis)
    came = swap(pick(value, at, 1 - me), axis).astype(jnp.float32)
    return (pick(value, at, me).astype(jnp.float32) + came).astype(value.dtype)


def copies(value, axes):
    return lax.all_to_all(jnp.broadcast_to(value, (lax.axis_size(axes), *value.shape)), axes, 0, 0, tiled=True)


def sums(value, axes):
    value = value.reshape(lax.axis_size(axes), -1, value.shape[-1])
    return jnp.sum(lax.all_to_all(value, axes, 0, 0, tiled=True).astype(jnp.float32), axis=0)


def padded(value, axis, size):
    widths = [(0, 0)] * value.ndim
    widths[axis] = (0, size - value.shape[axis])
    return jnp.pad(value, widths)


def fence(*values):
    return lax.optimization_barrier(values)


def mlp_kernel(units, act_ref, grad_ref, weight_ref, rows_out, hidden_out, part_out):
    both = raw_dot(act_ref[...], weight_ref[:, : 2 * units], NN)
    hidden_grad = raw_dot(grad_ref[...], weight_ref[:, 2 * units :], NN)
    gate, up = both[:, :units], both[:, units:]
    sigmoid_gate = jax.nn.sigmoid(gate)
    silu_gate = gate * sigmoid_gate
    hidden_out[...] = (silu_gate * up).astype(jnp.bfloat16)
    rows_out[:, :units] = (hidden_grad * up * sigmoid_gate * (1.0 + gate * (1.0 - sigmoid_gate))).astype(jnp.bfloat16)
    rows_out[:, units:] = (hidden_grad * silu_gate).astype(jnp.bfloat16)
    part_out[...] = raw_dot(rows_out[...], weight_ref[:, : 2 * units], NT).astype(jnp.bfloat16)


def mlp_of(act, grad, weight):
    tokens, width = act.shape
    units = weight.shape[1] // 3
    outs = [matrix(tokens, 2 * units, jnp.bfloat16), matrix(tokens, units, jnp.bfloat16), matrix(tokens, width, jnp.bfloat16)]
    return pl.pallas_call(
        functools.partial(mlp_kernel, units),
        in_specs=[whole_spec()] * 3,
        out_specs=[whole_spec()] * 3,
        out_shape=outs,
        compiler_params=settings(),
        cost_estimate=cost(1, 1),
        name="mlp",
    )(act, grad, weight)


def mlp_grads_kernel(act_ref, grad_ref, rows_ref, hidden_ref, out):
    wide = rows_ref.shape[1]
    out[:, :wide] = raw_dot(act_ref[...], rows_ref[...], TN).astype(jnp.bfloat16)
    out[:, wide:] = raw_dot(grad_ref[...], hidden_ref[...], TN).astype(jnp.bfloat16)


def mlp_grads_of(act, grad, rows, hidden):
    tokens, width = act.shape
    units = hidden.shape[1]
    step = width // 2
    column = pl.BlockSpec((tokens, step), lambda i: (0, i))
    return pl.pallas_call(
        mlp_grads_kernel,
        grid=(width // step,),
        in_specs=[column, column, plain_spec(rows.shape), plain_spec(hidden.shape)],
        out_specs=pl.BlockSpec((step, 3 * units), lambda i: (i, 0)),
        out_shape=matrix(width, 3 * units, jnp.bfloat16),
        compiler_params=settings(),
        cost_estimate=cost(1, 1),
        name="mlp_grads",
    )(act, grad, rows, hidden)


GRAD_ROWS = 3 * LEAF


def pair_grads_kernel(rows, in_ref, grad_ref, weight_ref, gain_ref, out, gain_out):
    result = raw_dot(in_ref[...], grad_ref[...], TN)
    beta = result[:, 4 * LEAF :].T[0:1, :]
    low = result[:, : 4 * LEAF].astype(jnp.bfloat16)
    bias = jnp.sum(grad_ref[:, 4 * LEAF :].astype(jnp.float32), axis=0, keepdims=True)
    wide = lambda x: jnp.concatenate([x, jnp.zeros((1, 4 * LEAF - x.shape[1]), jnp.float32)], axis=1)
    small = jnp.concatenate([wide(beta), wide(bias), jnp.zeros((EXTRA - 2, 4 * LEAF), jnp.float32)], axis=0).astype(jnp.bfloat16)
    for i in range(GRAD_ROWS // rows):
        out[i, :rows, :] = low[i * rows : (i + 1) * rows, :]
        out[i, rows:, :] = small
    products = jnp.sum(result * weight_ref[...].astype(jnp.float32), axis=1, keepdims=True)
    gain_out[...] = jnp.broadcast_to(products, (GRAD_ROWS, LEAF)).T[0:1, :] / gain_ref[...]


def pair_grads_of(attn_in, proj_grad, weight, gain, rows):
    length, width = attn_in.shape
    owners = GRAD_ROWS // rows
    row = pl.BlockSpec((1, GRAD_ROWS), lambda i: (0, i))
    return pl.pallas_call(
        functools.partial(pair_grads_kernel, rows),
        grid=(width // GRAD_ROWS,),
        in_specs=[
            pl.BlockSpec((length, GRAD_ROWS), lambda i: (0, i)),
            plain_spec(proj_grad.shape),
            pl.BlockSpec((GRAD_ROWS, weight.shape[1]), lambda i: (i, 0)),
            row,
        ],
        out_specs=[pl.BlockSpec((owners, rows + EXTRA, 4 * LEAF), lambda i: (i, 0, 0)), row],
        out_shape=[
            jax.ShapeDtypeStruct((width // rows, rows + EXTRA, 4 * LEAF), jnp.bfloat16),
            jax.ShapeDtypeStruct((1, width), jnp.float32),
        ],
        compiler_params=settings(),
        cost_estimate=cost(12 * 10**9, 36 * 10**6),
        name="pair_grads",
    )(attn_in, proj_grad, weight, gain.reshape(1, width))


def local(
    steps, tokens, w_query, w_key, w_value, w_house, w_beta, beta_bias, w_out, w_gate, w_up, w_down, gain_attn, gain_mlp, segment_ids, out_grad
):
    outer_axes, inner_axes = steps[:-2], steps[-2:]
    group = ("head", *inner_axes)
    low = jnp.bfloat16
    batches, positions, width = tokens.shape
    half = lax.axis_index("head")
    rank = lax.axis_index(steps)
    count = lax.axis_size(steps)
    inner = lax.axis_size(inner_axes)
    rows, half_heads = w_beta.shape
    assert batches == lax.axis_size("head") == 2 and 2 * half_heads <= count
    length = count * positions
    units = w_gate.shape[1] // inner
    depth = inner * rows
    scale = LEAF ** (-0.5)
    by_half = lambda own, other, at=0: by_index(own, other, "head", at)

    def gathered_outer(value):
        return lax.all_gather(value, outer_axes, axis=0, tiled=True)

    def to_owner(value):
        return exchanged(value.reshape(2, 2, rows, -1), inner_axes).reshape(inner, rows, -1)

    def outer_sums(value):
        return lax.psum_scatter(value, outer_axes, scatter_dimension=0, tiled=True)

    micro = lax.axis_index(steps[0])
    slots = count // 2
    four = (w_query, w_key, w_value, w_house)
    packed = jnp.stack(
        [jnp.concatenate([w[:, i * LEAF : (i + 1) * LEAF] for w in four], axis=1) for i in range(half_heads)]
    )
    beta_row = padded(w_beta.T[:, None, :], 2, 4 * LEAF)
    label_row = jnp.broadcast_to(padded(segment_ids.astype(low).reshape(1, 1, -1), 2, 4 * LEAF), (half_heads, 1, 4 * LEAF))
    packed = padded(padded(jnp.concatenate([packed, beta_row, label_row], axis=1), 1, rows + EXTRA), 0, slots)
    packed = jnp.broadcast_to(packed[None], (2, *packed.shape)).reshape(count, rows + EXTRA, 4 * LEAF)
    both_inputs = tokens.astype(jnp.float32)
    attn_in = exchanged((normalize(both_inputs) * gain_attn).astype(low), steps[:1])
    attn_in = lax.all_gather(attn_in, steps[1:], axis=1, tiled=True).reshape(length, width)
    blocks = [slice(i * units, (i + 1) * units) for i in range(inner)]
    mlp_own = jnp.stack([jnp.concatenate([w_gate[:, i], w_up[:, i], w_down[i].T], axis=1) for i in blocks])
    mlp_own = exchanged(mlp_own.reshape(2, 2, rows, 3 * units), inner_axes[:1])
    out_own = gathered(w_out.T, outer_axes)

    packed, mlp_own, out_own = fence(packed, mlp_own, out_own)

    packed = lax.all_to_all(packed, steps, 0, 0, tiled=True)
    mlp_own = exchange_at(mlp_own, 1, inner_axes[1]).reshape(depth, 3 * units)
    weight = packed[:, :rows].reshape(width, 4 * LEAF)
    beta_column = padded(packed[:, rows, :rows].reshape(width, 1), 1, LEAF)
    weight = jnp.concatenate([weight, beta_column], axis=1)
    label_all = pick(packed[:, rows + 1, : 2 * positions].reshape(count, 2, positions), 1, micro)
    label_all = label_all.reshape(1, length).astype(jnp.float32)
    label_column = jnp.broadcast_to(label_all.reshape(length, 1), (length, LEAF))
    weight, label_all, label_column, attn_in, mlp_own, out_own = fence(
        weight, label_all, label_column, attn_in, mlp_own, out_own
    )

    bias_row = padded(lax.dynamic_slice(padded(beta_bias, 0, slots), (rank % slots,), (1,)), 0, LEAF)
    bias_row = jnp.concatenate([jnp.zeros(4 * LEAF, jnp.float32), bias_row])
    proj = dot(attn_in, weight) + bias_row
    mlp_weight = gathered_outer(mlp_own)
    proj, out_own = fence(proj, out_own)

    out_own = gather_at(out_own, len(outer_axes), inner_axes[0])
    *saved, own_logits, query_moved, key_moved, product = leaf_forward(proj)
    own_logits, out_own = fence(own_logits, out_own)

    out_own = gather_at(out_own, len(outer_axes) + 1, inner_axes[1])
    attended, attended_low, log_total, *levels = run_merge_forward(
        proj, own_logits, query_moved, key_moved, product, label_column, label_all, scale
    )
    attended_low, out_own = fence(attended_low, out_own)
    out_own = out_own.reshape(width, half_heads * LEAF)

    grad_group = gather_at(gather_at(after(out_grad, attended_low), 1, inner_axes[0]), 2, inner_axes[1]).reshape(-1, width)
    heads_here = lax.all_to_all(attended_low.reshape(count, positions, LEAF), steps, 0, 0, tiled=True)
    heads_here = heads_here.reshape(2, slots, positions, LEAF)[:, :half_heads].transpose(0, 2, 1, 3)
    heads_here = heads_here.reshape(2 * positions, half_heads * LEAF)
    branch = dot(heads_here, out_own, NT).reshape(2, positions, width)
    branch = pick(branch, 0, half) + swap(pick(branch, 0, 1 - half).astype(low), "head").astype(jnp.float32)
    inputs = pick(tokens, 0, half).astype(jnp.float32)
    middle = inputs + branch
    normed_two = normalize(middle)
    mlp_in = (normed_two * gain_mlp).astype(low)
    mlp_group = copies(mlp_in, group).reshape(-1, width)
    columns = heads_here.reshape(2 * positions, inner, -1).transpose(1, 0, 2)
    columns = columns.reshape(2, 2, 2 * positions, -1)
    mlp_group, mlp_weight, grad_group = fence(mlp_group, mlp_weight, grad_group)

    rows_grad, hidden, mlp_in_part = mlp_of(mlp_group, grad_group, mlp_weight)
    mlp_in_grad = sums(mlp_in_part, group)
    mlp_grads = mlp_grads_of(mlp_group, grad_group, rows_grad, hidden)
    mlp_sums = outer_sums(mlp_grads)
    mlp_part = dot(hidden, mlp_weight[:, 2 * units :], NT).astype(low)
    columns = exchange_at(after(columns, mlp_grads), 0, inner_axes[0])
    mlp_in_grad, mlp_part, columns, mlp_grads = fence(mlp_in_grad, mlp_part, columns, mlp_grads)

    mlp_gain_part = jnp.sum(mlp_in_grad * normed_two, axis=0)
    own_grad = pick(out_grad, 0, half).astype(jnp.float32)
    middle_grad = own_grad + norm_back(mlp_in_grad * gain_mlp, normed_two, middle)
    branch_low = middle_grad.astype(low)
    branch_low = by_half(branch_low, swap(branch_low, "head"))
    attended_grad = dot(branch_low.reshape(2 * positions, width), out_own).astype(low)
    attended_grad = attended_grad.reshape(2, positions, half_heads, LEAF).transpose(0, 2, 1, 3)
    attended_grad = padded(attended_grad, 1, slots).reshape(count, positions, LEAF)
    attended_grad = lax.all_to_all(attended_grad, steps, 0, 0, tiled=True).reshape(length, LEAF).astype(jnp.float32)
    attended_grad, branch_low, mlp_part = fence(attended_grad, branch_low, mlp_part)

    mlp_part = scatter_at(mlp_part.reshape(2, 2, 2, positions, width), 0, "head")
    merged = run_merge_backward(
        proj, own_logits, query_moved, key_moved, product, levels, label_column, label_all, attended, log_total, attended_grad, scale
    )
    branch_group = gather_at(branch_low, 1, inner_axes[0])
    mlp_part, mlp_sums, branch_group, *merged = fence(mlp_part, mlp_sums, branch_group, *merged)

    mlp_part = scatter_at(mlp_part, 1, inner_axes[1])
    mlp_sums = exchange_at(mlp_sums.reshape(2, 2, rows, 3 * units), 0, inner_axes[0])
    middle_both = by_half(middle_grad, swap(middle_grad, "head"))
    proj_grad = leaf_backward(proj, saved, merged)
    branch_group = gather_at(branch_group, 2, inner_axes[1]).reshape(-1, width)
    proj_grad, mlp_part, middle_both, mlp_sums, branch_group = fence(proj_grad, mlp_part, middle_both, mlp_sums, branch_group)

    attn_in_part = dot(proj_grad, weight, NT).astype(low).reshape(*(2,) * len(steps), positions, width)
    packed_grad, attn_gain_part = pair_grads_of(attn_in, proj_grad, weight, gain_attn, rows)
    attn_in_part = scatter_at(attn_in_part, len(steps) - 1, steps[-1])
    mlp_grads = exchange_at(mlp_sums, 1, inner_axes[1]).reshape(inner, rows, 3 * units)
    mlp_part = scatter_at(mlp_part, 0, inner_axes[0])
    columns = exchange_at(columns, 1, inner_axes[1]).reshape(inner, 2, positions, -1)
    packed_grad, attn_gain_part, attn_in_part, mlp_grads, mlp_part, columns = fence(
        packed_grad, attn_gain_part, attn_in_part, mlp_grads, mlp_part, columns
    )

    packed_grad = lax.all_to_all(packed_grad, steps, 0, 0, tiled=True)
    attn_in_part = scatter_at(attn_in_part, 0, "head")
    for at in range(len(steps) - 2, 0, -1):
        attn_in_part = scatter_at(attn_in_part, at - 1, steps[at])
    gains = jnp.stack([attn_gain_part[0], mlp_gain_part])
    for axis in (*inner_axes, "head"):
        gains = gains + swap(gains, axis)
    columns = columns.swapaxes(0, 1).reshape(-1, columns.shape[-1])
    out_weight_grad = dot(branch_group, columns, TN).astype(low).reshape(count, rows, -1)
    mlp_grads = mlp_grads.astype(jnp.float32)
    gate_grad, up_grad = (
        mlp_grads[:, :, i * units : (i + 1) * units].transpose(1, 0, 2).reshape(rows, inner * units) for i in range(2)
    )
    down_grad = mlp_grads[:, :, 2 * units :].transpose(0, 2, 1).reshape(inner * units, rows)
    packed_grad, attn_in_part, mlp_part, gains, out_weight_grad, gate_grad, up_grad, down_grad = fence(
        packed_grad, attn_in_part, mlp_part, gains, out_weight_grad, gate_grad, up_grad, down_grad
    )

    plane = (steps[0], "head")
    same = lax.ppermute(attn_in_part, plane, [(0, 0), (1, 2), (2, 1), (3, 3)])
    opposite = lax.ppermute(attn_in_part, plane, [(0, 1), (1, 3), (2, 0), (3, 2)])
    attn_in_grad = by_half(same, opposite).astype(jnp.float32)

    block_out = (middle + mlp_part).astype(low)
    block_out = by_half(block_out, swap(block_out, "head"))
    out_weight_grad = lax.all_to_all(out_weight_grad, steps, 0, 0, tiled=True).astype(jnp.float32)
    out_weight_grad = jnp.sum(out_weight_grad.reshape(-1, inner, rows, out_weight_grad.shape[-1]), axis=0)
    out_weight_grad = out_weight_grad.transpose(0, 2, 1).reshape(-1, rows)

    for axis in outer_axes:
        gains = gains + swap(gains, axis)
    small = after(packed_grad[:, rows : rows + 2], gains)
    small = jnp.sum(small.reshape(2, slots, 2, -1)[:, :half_heads].astype(jnp.float32), axis=0)
    turn = rank % (GRAD_ROWS // rows) * rows
    beta_grad = lax.dynamic_slice(small[:, 0], (0, turn), (half_heads, rows)).T
    bias_grad = small[:, 1, 0]
    total = packed_grad[:, :rows].reshape(2, slots, rows, -1)[:, :half_heads].astype(jnp.float32)
    total = total[0] + total[1]
    grads = [total[..., i * LEAF : (i + 1) * LEAF].transpose(1, 0, 2).reshape(rows, half_heads * LEAF) for i in range(4)]

    attn_in_grad, *grads = fence(attn_in_grad, *grads)
    tokens_grad = middle_both + norm_back(attn_in_grad * gain_attn, normalize(both_inputs), both_inputs)
    return (
        block_out, tokens_grad, *grads, beta_grad, bias_grad, out_weight_grad, gate_grad, up_grad, down_grad, gains[0], gains[1]
    )


def solution(mesh):
    depth = mesh.shape["seq"].bit_length() - 1
    assert mesh.shape["seq"] == 2**depth and mesh.shape["head"] == 2
    steps = tuple(f"s{i}" for i in range(depth))
    fine = Mesh(mesh.devices.reshape(*(2,) * depth, 2), (*steps, "head"))
    split_rows, split_columns, by_position = P(steps, "head"), P("head", steps), P(None, steps, None)
    placed = (
        (by_position,) + (split_rows,) * 5 + (P("head"), split_columns, split_rows, split_rows, split_columns)
        + (P(), P(), P(None, steps), by_position)
    )
    returned = (
        (by_position, by_position) + (split_rows,) * 5 + (P("head"), split_columns, split_rows, split_rows, split_columns, P(), P())
    )
    return jax.shard_map(functools.partial(local, steps), mesh=fine, in_specs=placed, out_specs=returned, check_vma=False)
```
